32 devices in a mesh: dp: 1, gx: 4 (over y, x), gy: 8 (over z, core).
Axes of the slice: x: 2, y: 2, z: 4, core: 2. Of those that a mesh axis runs over, the one named last changes fastest.
Arguments:
- fields: float32 [1, 20, 16, 16, 512], P('dp', None, 'gx', 'gy'), may hold values from -6 to 6
- cotangent: float32 [1, 20, 16, 16, 512], P('dp', None, 'gx', 'gy'), may hold values from -6 to 6
- spectral: float32 [2, 144, 8, 12, 20, 20], P(None, 'gx', 'gy'), may hold values from -6 to 6
- bypass: float32 [20, 20], replicated, may hold values from -1.25 to 1.25
Outputs:
- outputs: float32 [1, 20, 16, 16, 512], P('dp', None, 'gx', 'gy')
- field_grad: float32 [1, 20, 16, 16, 512], P('dp', None, 'gx', 'gy')
- spectral_grad: float32 [2, 144, 8, 12, 20, 20], P(None, 'gx', 'gy')
The draws below stay inside these ranges and needn't reach their ends.
All inputs are finite; a program needn't handle non-finite values.
Results may differ from the reference program's by a relative error of at most 0.00011.
Values sent between devices are 32-bit elements; how exact they have to be, the bound alone decides.
A program may use at most 64 MiB of HBM per device.

```python
import math
import jax
import jax.numpy as jnp
from jax import lax

WIDTH = 20
DEPTH = 64
STEPS = 8
MODES_X = 12
MODES_Y = 12
MODES_Z = 12
MODES_T = 8
NXG = 16
NYG = 16
ZT = 512
MZT = 96
MZT_PART = 12
QY = 144
BATCH = 1
N_GY = 8


def levels(stream_key, shape, cuts, smallest, high):
    level, own = 1.0, jax.random.fold_in(stream_key, 6)
    for position, shards_of in cuts:
        steps = jnp.exp(jax.random.uniform(jax.random.fold_in(own, position), (shards_of,), jnp.float32, smallest / len(cuts), high / len(cuts)))
        level = level * jnp.repeat(steps, shape[position] // shards_of).reshape([-1 if axis == position else 1 for axis in range(len(shape))])
    return level


def gaussian(own_key, extent, scale, most, pieces=(), kind=jnp.bfloat16):
    values = scale * jax.random.normal(own_key, extent, jnp.float32)
    if pieces:
        values = values * levels(own_key, extent, pieces, -0.22, 0.18)
    return jnp.clip(values, -most, most).astype(kind)


def setup_inputs(seed: int = 0) -> dict:
    keys = jax.random.split(jax.random.key(seed), 5)
    return {
        "fields": gaussian(keys[0], (BATCH, WIDTH, NXG, NYG, ZT), 1.0, 6.0, ((2, 4), (3, 8)), jnp.float32),
        "cotangent": gaussian(keys[1], (BATCH, WIDTH, NXG, NYG, ZT), 1.0, 6.0, ((2, 4), (3, 8)), jnp.float32),
        "spectral": gaussian(keys[2], (2, QY, N_GY, MODES_X, WIDTH, WIDTH), 1.0, 6.0, ((1, 4), (2, 8)), jnp.float32),
        "bypass": gaussian(keys[3], (WIDTH, WIDTH), WIDTH ** -0.5, 1.25, (), jnp.float32),
    }


exact_mode = lax.Precision.HIGHEST

def frequencies(amount):
    indices = jnp.arange(amount, dtype=jnp.int32)
    return jnp.where(indices < amount // 2, indices, indices - amount)

def phases(freqs, positions, length):
    windings = freqs[:, None] * positions[None, :] % length
    angles = windings.astype(jnp.float32) * (2.0 * math.pi / length)
    return (jnp.cos(angles), jnp.sin(angles))

def depth_table(depth_cells, step_cells, modes_depth, modes_time):
    cell_ids = jnp.arange(depth_cells * step_cells, dtype=jnp.int32)
    mode_ids = jnp.arange(modes_depth * modes_time, dtype=jnp.int32)
    first = mode_ids // modes_time
    second = mode_ids % modes_time
    freq_z = jnp.where(first < modes_depth // 2, first, first - modes_depth)
    freq_t = jnp.where(second < modes_time // 2, second, second - modes_time)
    depth_pos = cell_ids // step_cells
    time_pos = cell_ids % step_cells
    windings = (freq_z[None, :] * depth_pos[:, None] * step_cells + freq_t[None, :] * time_pos[:, None] * depth_cells) % (depth_cells * step_cells)
    angles = windings.astype(jnp.float32) * (2.0 * math.pi / (depth_cells * step_cells))
    return (jnp.cos(angles), jnp.sin(angles))

def rotate_sum(pattern, cosine, sines, real_part, imag_part, sign):
    cos_real = jnp.einsum(pattern, cosine, real_part, precision=exact_mode)
    cos_imag = jnp.einsum(pattern, cosine, imag_part, precision=exact_mode)
    sin_real = jnp.einsum(pattern, sines, real_part, precision=exact_mode)
    sin_imag = jnp.einsum(pattern, sines, imag_part, precision=exact_mode)
    return (cos_real - sign * sin_imag, cos_imag + sign * sin_real)

def reference(fields, cotangent, spectral, bypass):
    cos_zt, sin_zt = depth_table(DEPTH, STEPS, MODES_Z, MODES_T)
    cos_y, sin_y = phases(frequencies(MODES_Y), jnp.arange(NYG, dtype=jnp.int32), NYG)
    cos_x, sin_x = phases(frequencies(MODES_X), jnp.arange(NXG, dtype=jnp.int32), NXG)
    cell_count = NXG * NYG * ZT

    def fourier_layer(sample, weights):
        depth_real = jnp.einsum('cxyr,rm->cxym', sample, cos_zt, precision=exact_mode)
        depth_imag = -jnp.einsum('cxyr,rm->cxym', sample, sin_zt, precision=exact_mode)
        along_real, along_imag = rotate_sum('ly,cxym->cxlm', cos_y, sin_y, depth_real, depth_imag, -1.0)
        spec_real, spec_imag = rotate_sum('kx,cxlm->clkm', cos_x, sin_x, along_real, along_imag, -1.0)
        weight_real = weights[0]
        weight_imag = weights[1]
        mixing = 'clkm,lkmco->olkm'
        mixed_real = jnp.einsum(mixing, spec_real, weight_real, precision=exact_mode) - jnp.einsum(mixing, spec_imag, weight_imag, precision=exact_mode)
        mixed_imag = jnp.einsum(mixing, spec_real, weight_imag, precision=exact_mode) + jnp.einsum(mixing, spec_imag, weight_real, precision=exact_mode)
        back_real, back_imag = rotate_sum('kx,olkm->olxm', cos_x, sin_x, mixed_real, mixed_imag, 1.0)
        cell_real, cell_imag = rotate_sum('ly,olxm->oxym', cos_y, sin_y, back_real, back_imag, 1.0)
        spectral_part = (jnp.einsum('oxym,rm->oxyr', cell_real, cos_zt, precision=exact_mode) - jnp.einsum('oxym,rm->oxyr', cell_imag, sin_zt, precision=exact_mode)) / cell_count
        pre = spectral_part + jnp.einsum('cxyr,co->oxyr', sample, bypass, precision=exact_mode)
        return jax.nn.gelu(pre)

    def objective(field_all, weight_all):
        shaped = weight_all.reshape(2, MODES_Y, MZT_PART, N_GY, MODES_X, WIDTH, WIDTH)
        shaped = jnp.transpose(shaped, (0, 1, 4, 3, 2, 5, 6)).reshape(2, MODES_Y, MODES_X, MZT, WIDTH, WIDTH)
        return lax.map(lambda sample: fourier_layer(sample, shaped), field_all)
    outputs, pullback = jax.vjp(objective, fields, spectral)
    field_grad, spectral_grad = pullback(cotangent)
    return (outputs, field_grad, spectral_grad)
```

```python
import functools
import math

import jax
import jax.numpy as jnp
import numpy as np
from jax import lax
from jax.experimental import pallas as pl
from jax.experimental.pallas import tpu as pltpu
from jax.sharding import PartitionSpec as P

STEPS = 8
MODES_X = 12
MODES_Y = 12
MODES_Z = 12
MODES_T = 8
LANES = 128
MESH = pl.DeviceIdType.MESH
close = lax.Precision.HIGH
NN = (((1,), (0,)), ((), ()))
NT = (((1,), (1,)), ((), ()))
TN = (((0,), (0,)), ((), ()))


def up(value, step):
    return -(-value // step) * step


def product(left, right, dims):
    return lax.dot_general(left, right, dims, precision=close, preferred_element_type=jnp.float32)


def signed(amount):
    ids = np.arange(amount)
    return np.where(ids < amount // 2, ids, ids - amount)


class Sizes:
    def __init__(self, sample, spectral, size_x, size_y):
        _, self.chan, self.rows_x, self.rows_y, self.cells = sample
        self.nx, self.ny = size_x, size_y
        self.full_x, self.full_y = self.rows_x * size_x, self.rows_y * size_y
        self.count = self.full_x * self.full_y * self.cells
        self.tiles = self.cells // LANES
        self.qb = spectral[1]
        self.kx = spectral[3]
        self.mb = MODES_Z * MODES_T // size_y
        self.ly = MODES_Y
        self.mb2 = up(2 * self.mb, 8)
        self.half = self.mb2 // 2
        self.cx = self.chan * self.rows_x
        self.cp = up(self.cx, LANES)
        self.kp = up(self.kx, 8)
        self.qbp = up(self.qb, 8)
        self.spec_rows = 2 * self.chan * self.kp

    def pieces(self, mode):
        start, stop, found = mode * self.mb, (mode + 1) * self.mb, []
        while start < stop:
            owner = start // self.qb
            rows = min(stop, (owner + 1) * self.qb) - start
            found.append((owner, start - owner * self.qb, start - mode * self.mb, rows))
            start += rows
        return found


def depth_table(z):
    depth = z.cells // STEPS
    modes = np.arange(MODES_Z * MODES_T)
    freq_z, freq_t = signed(MODES_Z)[modes // MODES_T], signed(MODES_T)[modes % MODES_T]
    cell = np.arange(z.cells)
    turns = freq_z[:, None] * (cell // STEPS) * STEPS + freq_t[:, None] * (cell % STEPS) * depth
    angle = (turns % z.cells) * (2.0 * math.pi / z.cells)
    table = np.zeros((z.ny, 2, z.half, z.cells))
    table[:, 0, : z.mb] = np.cos(angle).reshape(z.ny, z.mb, z.cells)
    table[:, 1, : z.mb] = -np.sin(angle).reshape(z.ny, z.mb, z.cells)
    return table.reshape(z.ny * z.mb2, z.cells).astype(np.float32)


def x_table(z):
    angle = (signed(z.kx)[:, None] * np.arange(z.full_x) % z.full_x) * (2.0 * math.pi / z.full_x)
    cosine = np.cos(angle).reshape(z.kx, z.nx, z.rows_x)
    sine = np.sin(angle).reshape(z.kx, z.nx, z.rows_x)
    table = np.zeros((2, z.chan, z.kp, z.nx, 2, z.cp))
    for c in range(z.chan):
        cols = slice(c * z.rows_x, (c + 1) * z.rows_x)
        table[0, c, : z.kx, :, 0, cols] = cosine
        table[0, c, : z.kx, :, 1, cols] = sine
        table[1, c, : z.kx, :, 0, cols] = -sine
        table[1, c, : z.kx, :, 1, cols] = cosine
    return table.reshape(z.spec_rows, z.nx * 2 * z.cp).astype(np.float32)


def chain(
    z, fields, cotangent, depth, bypass, spread, same_x, w_hbm, x_hbm,
    output, field_grad, spec, dual,
    w, xt, unit, mixed, signal, direct, sg, rg, sx, rx, gs, gr, xs, xr, wsem, xsem,
):
    me_x, me_y = lax.axis_index("gx"), lax.axis_index("gy")
    axes = {"gx": (me_x, z.nx), "gy": (me_y, z.ny)}

    barrier = pltpu.get_barrier_semaphore()
    for axis, (me, n) in axes.items():
        for step in range(1, n):
            pl.semaphore_signal(
                barrier, inc=1, device_id={axis: lax.rem(me + step, n)}, device_id_type=MESH
            )
    load_x = pltpu.make_async_copy(x_hbm, xt, xsem)
    load_x.start()
    load_w = pltpu.make_async_copy(w_hbm, w, wsem)
    load_w.start()

    def send(axis, src, dst, send_sem, recv_sem):
        me, n = axes[axis]
        copies = []
        for step in range(1, n):
            peer = lax.rem(me + step, n)
            copy = pltpu.make_async_remote_copy(
                src_ref=src.at[peer],
                dst_ref=dst.at[me],
                send_sem=send_sem.at[step],
                recv_sem=recv_sem.at[step],
                device_id={axis: peer},
                device_id_type=MESH,
            )
            copy.start()
            copies.append(copy)
        dst[me] = src[me]
        return copies

    def send_y(turn):
        return send("gy", sg.at[turn], rg.at[turn], gs.at[turn], gr.at[turn])

    def send_x(turn):
        return send("gx", sx.at[turn], rx.at[turn], xs.at[turn], xr.at[turn])

    def finish(copies):
        for copy in copies:
            copy.wait()

    stride = z.tiles * z.rows_y

    def cells_of(ref, y):
        parts = [ref[pl.ds(t * z.rows_y + y, z.cx, stride=stride), :] for t in range(z.tiles)]
        return jnp.concatenate(parts, axis=1)

    def put_cells(ref, y, value):
        for t in range(z.tiles):
            ref[pl.ds(t * z.rows_y + y, z.cx, stride=stride), :] = value[:, t * LANES : (t + 1) * LANES]

    def lanes(y):
        return slice((y % z.rows_y) * z.cp, (y % z.rows_y + 1) * z.cp)

    def depth_in(turn, y, cells):
        if z.cp > z.cx:
            cells = jnp.concatenate([cells, jnp.zeros((z.cp - z.cx, z.cells), jnp.float32)], axis=0)
        found = product(depth[...], cells, NT)
        for block in range(z.ny):
            sg[turn, block, :, lanes(y)] = found[block * z.mb2 : (block + 1) * z.mb2]

    def depth_out(turn, y):
        held = rg[turn, :, :, lanes(y)].reshape(z.ny * z.mb2, z.cp)
        return product(held, depth[...], TN)[: z.cx]

    first_half = lax.broadcasted_iota(jnp.int32, (z.mb2, z.cp), 0) < z.half
    minus_i = jnp.where(first_half, 1.0, -1.0)

    def times_minus_i(value):
        return pltpu.roll(value, z.half, 0) * minus_i

    def wave(y, f):
        angle = 2.0 * math.pi * ((y * f) % z.full_y) / z.full_y
        return math.cos(angle), math.sin(angle)

    def total(terms):
        out = None
        for factor, value in terms:
            if abs(factor) < 1e-12:
                continue
            term = value if factor == 1.0 else value * factor
            out = term if out is None else out + term
        return out

    mid, top = z.full_y // 2, z.ly // 2

    def y_in(turn):
        at = [rg[turn, y // z.rows_y, :, lanes(y)] for y in range(z.full_y)]
        even = [at[y] if y in (0, mid) else at[y] + at[z.full_y - y] for y in range(mid + 1)]
        odd = [None if y in (0, mid) else at[y] - at[z.full_y - y] for y in range(mid)]

        def put(mode, value):
            for part in range(2):
                for owner, there, here, rows in z.pieces(mode):
                    low, base = part * z.half + here, part * z.qbp + there
                    sx[turn, owner, base : base + rows, :] = value[low : low + rows]

        for f in range(top + 1):
            cosines = total([(wave(y, f)[0], even[y]) for y in range(mid + 1)])
            if f == 0:
                put(0, cosines)
                continue
            sines = times_minus_i(total([(wave(y, f)[1], odd[y]) for y in range(1, mid)]))
            if f < top:
                put(f, cosines + sines)
            put(z.ly - f, cosines - sines)

    def y_out(turn):
        for mode in range(z.ly):
            for part in range(2):
                for owner, there, here, rows in z.pieces(mode):
                    low, base = part * z.half + here, part * z.qbp + there
                    unit[mode, low : low + rows, :] = rx[turn, owner, base : base + rows, :]
        even, odd = [unit[0]], [None]
        for f in range(1, top + 1):
            back = unit[z.ly - f]
            ahead = unit[f] if f < top else None
            even.append(back if ahead is None else ahead + back)
            odd.append(times_minus_i(back if ahead is None else back - ahead))
        for y in range(mid + 1):
            cosines = total([(wave(y, f)[0], even[f]) for f in range(top + 1)])
            sines = total([(wave(y, f)[1], odd[f]) for f in range(1, top + 1)]) if 0 < y < mid else None
            if sines is None:
                sg[turn, y // z.rows_y, :, lanes(y)] = cosines
                continue
            other = z.full_y - y
            sg[turn, y // z.rows_y, :, lanes(y)] = cosines + sines
            sg[turn, other // z.rows_y, :, lanes(other)] = cosines - sines

    def x_in(turn):
        held = [
            rx[turn, s, part * z.qbp : part * z.qbp + z.qb, :]
            for s in range(z.nx)
            for part in range(2)
        ]
        return product(xt[...], jnp.concatenate(held, axis=1), NT)

    def x_out(turn):
        found = product(mixed[...], xt[...], TN)
        for s in range(z.nx):
            for part in range(2):
                col = (2 * s + part) * z.cp
                sx[turn, s, part * z.qbp : part * z.qbp + z.qb, :] = found[:, col : col + z.cp]

    pairs = z.chan * z.chan

    def weight(part, row):
        return w[pl.ds(part * z.kx * pairs + row, z.kx, stride=pairs), :]

    def modes(ref, part, channel):
        return ref[pl.ds(pl.multiple_of((part * z.chan + channel) * z.kp, 8), z.kx), :]

    def mix(source, adjoint, scale):
        sign = -1.0 if adjoint else 1.0

        def body(to, carry):
            real = jnp.zeros((z.kx, z.qb), jnp.float32)
            imag = jnp.zeros((z.kx, z.qb), jnp.float32)
            for c in range(z.chan):
                row = to * z.chan + c if adjoint else c * z.chan + to
                w_real, w_imag = weight(0, row), weight(1, row)
                s_real, s_imag = modes(source, 0, c), modes(source, 1, c)
                real = real + s_real * w_real - sign * (s_imag * w_imag)
                imag = imag + s_imag * w_real + sign * (s_real * w_imag)
            for part, value in ((0, real), (1, imag)):
                at = pl.multiple_of((part * z.chan + to) * z.kp, 8)
                mixed[pl.ds(at, z.kx), :] = value if scale is None else value * scale
            return carry

        lax.fori_loop(0, z.chan, body, 0)

    for y in range(z.rows_y):
        depth_in(0, y, cells_of(fields, y))
    pl.semaphore_wait(barrier, z.nx + z.ny - 2)
    moving = send_y(0)
    mixed[...] = jnp.zeros_like(mixed)
    if z.half != z.mb:
        unit[...] = jnp.zeros_like(unit)
    exact = lax.Precision.HIGHEST
    wide = lax.dot_general(spread[...], bypass[...], NN, precision=exact)
    square = lax.dot_general(wide, spread[...], NT, precision=exact) * same_x[...]
    for y in range(z.rows_y):
        direct[y] = product(square, cells_of(fields, y), TN)
    finish(moving)
    y_in(0)
    moving = send_x(0)
    load_x.wait()
    finish(moving)
    spec[...] = x_in(0)
    load_w.wait()
    mix(spec, False, 1.0 / z.count)
    x_out(1)
    finish(send_x(1))
    y_out(1)
    finish(send_y(1))

    root = math.sqrt(2.0 / math.pi)
    for y in range(z.rows_y):
        pre = depth_out(1, y) + direct[y]
        square_pre = pre * pre
        bend = jnp.tanh(root * (pre + 0.044715 * (square_pre * pre)))
        put_cells(output, y, 0.5 * pre * (1.0 + bend))
        slope = 0.5 * (1.0 + bend) + 0.5 * pre * (1.0 - bend * bend) * (
            root * (1.0 + 3.0 * 0.044715 * square_pre)
        )
        back = cells_of(cotangent, y) * slope
        signal[y] = back
        depth_in(2, y, back)

    moving = send_y(2)
    for y in range(z.rows_y):
        direct[y] = product(square, signal[y], NN)
    finish(moving)
    y_in(2)
    finish(send_x(2))
    dual[...] = x_in(2) * (1.0 / z.count)
    mix(dual, True, None)
    x_out(3)
    finish(send_x(3))
    y_out(3)
    finish(send_y(3))
    for y in range(z.rows_y):
        put_cells(field_grad, y, depth_out(3, y) + direct[y])


def outer(z, block, spec, dual, grad):
    part = pl.program_id(0)
    sign = (1 - 2 * part).astype(jnp.float32)
    pairs = z.chan * z.chan
    for k in range(block):
        kx = pl.program_id(1) * block + k
        same = dual[pl.ds(part * z.chan * z.kp + kx, z.chan, stride=z.kp), :]
        cross = dual[pl.ds((1 - part) * z.chan * z.kp + kx, z.chan, stride=z.kp), :] * sign
        for c in range(z.chan):
            real = spec[pl.ds(c * z.kp + kx, 1), :]
            imag = spec[pl.ds((z.chan + c) * z.kp + kx, 1), :]
            at = k * pairs + c * z.chan
            grad[at : at + z.chan, :] = real * same + imag * cross


def on_device(fields, cotangent, spectral, bypass):
    z = Sizes(fields.shape, spectral.shape, lax.axis_size("gx"), lax.axis_size("gy"))
    f32 = jnp.float32

    def rows(value):
        shaped = value.reshape(z.chan, z.rows_x, z.rows_y, z.tiles, LANES)
        return shaped.transpose(0, 1, 3, 2, 4).reshape(-1, LANES)

    def unrows(value):
        shaped = value.reshape(z.chan, z.rows_x, z.tiles, z.rows_y, LANES)
        return shaped.transpose(0, 1, 3, 2, 4).reshape(fields.shape)

    weights = spectral.transpose(0, 3, 4, 5, 2, 1).reshape(-1, z.qb)
    spread = np.kron(np.eye(z.chan), np.ones((z.rows_x, 1))).astype(np.float32)
    same_x = np.kron(np.ones((z.chan, z.chan)), np.eye(z.rows_x)).astype(np.float32)
    x_cols = z.nx * 2 * z.cp
    vmem = pl.BlockSpec(memory_space=pltpu.VMEM)
    hbm = pl.BlockSpec(memory_space=pl.ANY)
    grid_rows = z.cx * z.rows_y * z.tiles
    y_block = (4, z.ny, z.mb2, z.rows_y * z.cp)
    x_block = (4, z.nx, 2 * z.qbp, z.cp)
    output, field_grad, spec, dual = pl.pallas_call(
        functools.partial(chain, z),
        out_shape=(
            jax.ShapeDtypeStruct((grid_rows, LANES), f32),
            jax.ShapeDtypeStruct((grid_rows, LANES), f32),
            jax.ShapeDtypeStruct((z.spec_rows, z.qb), f32),
            jax.ShapeDtypeStruct((z.spec_rows, z.qb), f32),
        ),
        in_specs=[vmem] * 6 + [hbm] * 2,
        out_specs=[vmem] * 4,
        scratch_shapes=[
            pltpu.VMEM(weights.shape, f32),
            pltpu.VMEM((z.spec_rows, x_cols), f32),
            pltpu.VMEM((z.ly, z.mb2, z.cp), f32),
            pltpu.VMEM((z.spec_rows, z.qb), f32),
            pltpu.VMEM((z.rows_y, z.cx, z.cells), f32),
            pltpu.VMEM((z.rows_y, z.cx, z.cells), f32),
            pltpu.VMEM(y_block, f32),
            pltpu.VMEM(y_block, f32),
            pltpu.VMEM(x_block, f32),
            pltpu.VMEM(x_block, f32),
            pltpu.SemaphoreType.DMA((4, z.ny)),
            pltpu.SemaphoreType.DMA((4, z.ny)),
            pltpu.SemaphoreType.DMA((4, z.nx)),
            pltpu.SemaphoreType.DMA((4, z.nx)),
            pltpu.SemaphoreType.DMA,
            pltpu.SemaphoreType.DMA,
        ],
        compiler_params=pltpu.CompilerParams(
            collective_id=0, has_side_effects=True, vmem_limit_bytes=48 << 20
        ),
        name="fourier_chain",
    )(
        rows(fields), rows(cotangent), depth_table(z), bypass, spread, same_x, weights, x_table(z)
    )
    block = 4 if z.kx % 4 == 0 else z.kx
    per_step = block * z.chan * z.chan
    local_grad = pl.pallas_call(
        functools.partial(outer, z, block),
        grid=(2, z.kx // block),
        out_shape=jax.ShapeDtypeStruct(weights.shape, f32),
        in_specs=[pl.BlockSpec((z.spec_rows, z.qb), lambda p, k: (0, 0))] * 2,
        out_specs=pl.BlockSpec((per_step, z.qb), lambda p, k: (p * (z.kx // block) + k, 0)),
        compiler_params=pltpu.CompilerParams(vmem_limit_bytes=16 << 20),
        name="outer_products",
    )(spec, dual)
    spectral_grad = local_grad.reshape(2, z.kx, z.chan, z.chan, 1, z.qb).transpose(0, 5, 4, 1, 2, 3)
    if lax.axis_size("dp") > 1:
        spectral_grad = lax.psum(spectral_grad, "dp")
    return (unrows(output), unrows(field_grad), spectral_grad)


def solution(mesh):
    cells = P("dp", None, "gx", "gy", None)
    weights = P(None, "gx", "gy", None, None, None)
    return jax.shard_map(
        on_device,
        mesh=mesh,
        in_specs=(cells, cells, weights, P()),
        out_specs=(cells, cells, weights),
        check_vma=False,
    )
```

```python
import functools
import math

import jax
import jax.numpy as jnp
import numpy as np
from jax import lax
from jax.experimental import pallas as pl
from jax.experimental.pallas import tpu as pltpu
from jax.sharding import PartitionSpec as P

STEPS = 8
MODES_X = 12
MODES_Y = 12
MODES_Z = 12
MODES_T = 8
LANES = 128
MESH = pl.DeviceIdType.MESH
close = lax.Precision.HIGH
NN = (((1,), (0,)), ((), ()))
NT = (((1,), (1,)), ((), ()))
TN = (((0,), (0,)), ((), ()))


def up(value, step):
    return -(-value // step) * step


def product(left, right, dims):
    return lax.dot_general(left, right, dims, precision=close, preferred_element_type=jnp.float32)


def signed(amount):
    ids = np.arange(amount)
    return np.where(ids < amount // 2, ids, ids - amount)


class Sizes:
    def __init__(self, sample, spectral, size_x, size_y):
        _, self.chan, self.rows_x, self.rows_y, self.cells = sample
        self.nx, self.ny = size_x, size_y
        self.full_x, self.full_y = self.rows_x * size_x, self.rows_y * size_y
        self.count = self.full_x * self.full_y * self.cells
        self.tiles = self.cells // LANES
        self.qb = spectral[1]
        self.kx = spectral[3]
        self.mb = MODES_Z * MODES_T // size_y
        self.ly = MODES_Y
        self.mb2 = up(2 * self.mb, 8)
        self.half = self.mb2 // 2
        self.cx = self.chan * self.rows_x
        self.cp = up(self.cx, LANES)
        self.kp = up(self.kx, 8)
        self.qbp = up(self.qb, 8)
        self.spec_rows = 2 * self.chan * self.kp

    def pieces(self, mode):
        start, stop, found = mode * self.mb, (mode + 1) * self.mb, []
        while start < stop:
            owner = start // self.qb
            rows = min(stop, (owner + 1) * self.qb) - start
            found.append((owner, start - owner * self.qb, start - mode * self.mb, rows))
            start += rows
        return found


def depth_table(z):
    depth = z.cells // STEPS
    modes = np.arange(MODES_Z * MODES_T)
    freq_z, freq_t = signed(MODES_Z)[modes // MODES_T], signed(MODES_T)[modes % MODES_T]
    cell = np.arange(z.cells)
    turns = freq_z[:, None] * (cell // STEPS) * STEPS + freq_t[:, None] * (cell % STEPS) * depth
    angle = (turns % z.cells) * (2.0 * math.pi / z.cells)
    table = np.zeros((z.ny, 2, z.half, z.cells))
    table[:, 0, : z.mb] = np.cos(angle).reshape(z.ny, z.mb, z.cells)
    table[:, 1, : z.mb] = -np.sin(angle).reshape(z.ny, z.mb, z.cells)
    return table.reshape(z.ny * z.mb2, z.cells).astype(np.float32)


def x_table(z):
    angle = (signed(z.kx)[:, None] * np.arange(z.full_x) % z.full_x) * (2.0 * math.pi / z.full_x)
    cosine = np.cos(angle).reshape(z.kx, z.nx, z.rows_x)
    sine = np.sin(angle).reshape(z.kx, z.nx, z.rows_x)
    table = np.zeros((2, z.chan, z.kp, z.nx, 2, z.cp))
    for c in range(z.chan):
        cols = slice(c * z.rows_x, (c + 1) * z.rows_x)
        table[0, c, : z.kx, :, 0, cols] = cosine
        table[0, c, : z.kx, :, 1, cols] = sine
        table[1, c, : z.kx, :, 0, cols] = -sine
        table[1, c, : z.kx, :, 1, cols] = cosine
    return table.reshape(z.spec_rows, z.nx * 2 * z.cp).astype(np.float32)


def chain(
    z, fields_hbm, cotangent_hbm, depth_hbm, bypass_hbm, spread_hbm, same_hbm, w_hbm, x_hbm,
    output_hbm, grad_hbm, spec_hbm, dual_hbm,
    output, field_grad, spec, dual, fields, cotangent, depth, bypass, spread, same_x, w, xt, unit, mixed, signal, direct, sg, rg, sx, rx, gs, gr, xs, xr, load_sems, store_sems,
):
    me_x, me_y = lax.axis_index("gx"), lax.axis_index("gy")
    axes = {"gx": (me_x, z.nx), "gy": (me_y, z.ny)}

    barrier = pltpu.get_barrier_semaphore()
    for axis, (me, n) in axes.items():
        for step in range(1, n):
            pl.semaphore_signal(
                barrier, inc=1, device_id={axis: lax.rem(me + step, n)}, device_id_type=MESH
            )
    loads = {}
    for name, src, dst in (
        ("depth", depth_hbm, depth),
        ("fields", fields_hbm, fields),
        ("bypass", bypass_hbm, bypass),
        ("spread", spread_hbm, spread),
        ("same_x", same_hbm, same_x),
        ("x", x_hbm, xt),
        ("w", w_hbm, w),
        ("cotangent", cotangent_hbm, cotangent),
    ):
        loads[name] = pltpu.make_async_copy(src, dst, load_sems.at[len(loads)])
        loads[name].start()

    stores = []

    def store(src, dst):
        stores.append(pltpu.make_async_copy(src, dst, store_sems.at[len(stores)]))
        stores[-1].start()

    def send(axis, src, dst, send_sem, recv_sem):
        me, n = axes[axis]
        copies = []
        for step in range(1, n):
            peer = lax.rem(me + step, n)
            copy = pltpu.make_async_remote_copy(
                src_ref=src.at[peer],
                dst_ref=dst.at[me],
                send_sem=send_sem.at[step],
                recv_sem=recv_sem.at[step],
                device_id={axis: peer},
                device_id_type=MESH,
            )
            copy.start()
            copies.append(copy)
        dst[me] = src[me]
        return copies

    def send_y(turn):
        return send("gy", sg.at[turn], rg.at[turn], gs.at[turn], gr.at[turn])

    def send_x(turn):
        return send("gx", sx.at[turn], rx.at[turn], xs.at[turn], xr.at[turn])

    def finish(copies):
        for copy in copies:
            copy.wait()

    stride = z.tiles * z.rows_y

    def cells_of(ref, y):
        parts = [ref[pl.ds(t * z.rows_y + y, z.cx, stride=stride), :] for t in range(z.tiles)]
        return jnp.concatenate(parts, axis=1)

    def put_cells(ref, y, value):
        for t in range(z.tiles):
            ref[pl.ds(t * z.rows_y + y, z.cx, stride=stride), :] = value[:, t * LANES : (t + 1) * LANES]

    def lanes(y):
        return slice((y % z.rows_y) * z.cp, (y % z.rows_y + 1) * z.cp)

    def depth_in(turn, y, cells):
        if z.cp > z.cx:
            cells = jnp.concatenate([cells, jnp.zeros((z.cp - z.cx, z.cells), jnp.float32)], axis=0)
        found = product(depth[...], cells, NT)
        for block in range(z.ny):
            sg[turn, block, :, lanes(y)] = found[block * z.mb2 : (block + 1) * z.mb2]

    def depth_out(turn, y):
        held = rg[turn, :, :, lanes(y)].reshape(z.ny * z.mb2, z.cp)
        return product(held, depth[...], TN)[: z.cx]

    first_half = lax.broadcasted_iota(jnp.int32, (z.mb2, z.cp), 0) < z.half
    minus_i = jnp.where(first_half, 1.0, -1.0)

    def times_minus_i(value):
        return pltpu.roll(value, z.half, 0) * minus_i

    def wave(y, f):
        angle = 2.0 * math.pi * ((y * f) % z.full_y) / z.full_y
        return math.cos(angle), math.sin(angle)

    def total(terms):
        out = None
        for factor, value in terms:
            if abs(factor) < 1e-12:
                continue
            term = value if factor == 1.0 else value * factor
            out = term if out is None else out + term
        return out

    mid, top = z.full_y // 2, z.ly // 2

    def y_in(turn):
        at = [rg[turn, y // z.rows_y, :, lanes(y)] for y in range(z.full_y)]
        even = [at[y] if y in (0, mid) else at[y] + at[z.full_y - y] for y in range(mid + 1)]
        odd = [None if y in (0, mid) else at[y] - at[z.full_y - y] for y in range(mid)]

        def put(mode, value):
            for part in range(2):
                for owner, there, here, rows in z.pieces(mode):
                    low, base = part * z.half + here, part * z.qbp + there
                    sx[turn, owner, base : base + rows, :] = value[low : low + rows]

        for f in range(top + 1):
            cosines = total([(wave(y, f)[0], even[y]) for y in range(mid + 1)])
            if f == 0:
                put(0, cosines)
                continue
            sines = times_minus_i(total([(wave(y, f)[1], odd[y]) for y in range(1, mid)]))
            if f < top:
                put(f, cosines + sines)
            put(z.ly - f, cosines - sines)

    def y_out(turn):
        for mode in range(z.ly):
            for part in range(2):
                for owner, there, here, rows in z.pieces(mode):
                    low, base = part * z.half + here, part * z.qbp + there
                    unit[mode, low : low + rows, :] = rx[turn, owner, base : base + rows, :]
        even, odd = [unit[0]], [None]
        for f in range(1, top + 1):
            back = unit[z.ly - f]
            ahead = unit[f] if f < top else None
            even.append(back if ahead is None else ahead + back)
            odd.append(times_minus_i(back if ahead is None else back - ahead))
        for y in range(mid + 1):
            cosines = total([(wave(y, f)[0], even[f]) for f in range(top + 1)])
            sines = total([(wave(y, f)[1], odd[f]) for f in range(1, top + 1)]) if 0 < y < mid else None
            if sines is None:
                sg[turn, y // z.rows_y, :, lanes(y)] = cosines
                continue
            other = z.full_y - y
            sg[turn, y // z.rows_y, :, lanes(y)] = cosines + sines
            sg[turn, other // z.rows_y, :, lanes(other)] = cosines - sines

    def x_in(turn):
        held = [
            rx[turn, s, part * z.qbp : part * z.qbp + z.qb, :]
            for s in range(z.nx)
            for part in range(2)
        ]
        return product(xt[...], jnp.concatenate(held, axis=1), NT)

    def x_out(turn):
        found = product(mixed[...], xt[...], TN)
        for s in range(z.nx):
            for part in range(2):
                col = (2 * s + part) * z.cp
                sx[turn, s, part * z.qbp : part * z.qbp + z.qb, :] = found[:, col : col + z.cp]

    pairs = z.chan * z.chan

    def weight(part, row):
        return w[pl.ds(part * z.kx * pairs + row, z.kx, stride=pairs), :]

    def modes(ref, part, channel):
        return ref[pl.ds(pl.multiple_of((part * z.chan + channel) * z.kp, 8), z.kx), :]

    def mix(source, adjoint, scale):
        sign = -1.0 if adjoint else 1.0

        def body(to, carry):
            real = jnp.zeros((z.kx, z.qb), jnp.float32)
            imag = jnp.zeros((z.kx, z.qb), jnp.float32)
            for c in range(z.chan):
                row = to * z.chan + c if adjoint else c * z.chan + to
                w_real, w_imag = weight(0, row), weight(1, row)
                s_real, s_imag = modes(source, 0, c), modes(source, 1, c)
                real = real + s_real * w_real - sign * (s_imag * w_imag)
                imag = imag + s_imag * w_real + sign * (s_real * w_imag)
            for part, value in ((0, real), (1, imag)):
                at = pl.multiple_of((part * z.chan + to) * z.kp, 8)
                mixed[pl.ds(at, z.kx), :] = value if scale is None else value * scale
            return carry

        lax.fori_loop(0, z.chan, body, 0)

    loads["depth"].wait()
    loads["fields"].wait()
    for y in range(z.rows_y):
        depth_in(0, y, cells_of(fields, y))
    pl.semaphore_wait(barrier, z.nx + z.ny - 2)
    moving = send_y(0)
    mixed[...] = jnp.zeros_like(mixed)
    if z.half != z.mb:
        unit[...] = jnp.zeros_like(unit)
    for name in ("bypass", "spread", "same_x"):
        loads[name].wait()
    exact = lax.Precision.HIGHEST
    wide = lax.dot_general(spread[...], bypass[...], NN, precision=exact)
    square = lax.dot_general(wide, spread[...], NT, precision=exact) * same_x[...]
    for y in range(z.rows_y):
        direct[y] = product(square, cells_of(fields, y), TN)
    finish(moving)
    y_in(0)
    moving = send_x(0)
    loads["x"].wait()
    finish(moving)
    spec[...] = x_in(0)
    loads["w"].wait()
    mix(spec, False, 1.0 / z.count)
    x_out(1)
    finish(send_x(1))
    y_out(1)
    finish(send_y(1))
    loads["cotangent"].wait()

    root = math.sqrt(2.0 / math.pi)
    for y in range(z.rows_y):
        pre = depth_out(1, y) + direct[y]
        square_pre = pre * pre
        bend = jnp.tanh(root * (pre + 0.044715 * (square_pre * pre)))
        put_cells(output, y, 0.5 * pre * (1.0 + bend))
        slope = 0.5 * (1.0 + bend) + 0.5 * pre * (1.0 - bend * bend) * (
            root * (1.0 + 3.0 * 0.044715 * square_pre)
        )
        back = cells_of(cotangent, y) * slope
        signal[y] = back
        depth_in(2, y, back)

    moving = send_y(2)
    store(spec, spec_hbm)
    store(output, output_hbm)
    for y in range(z.rows_y):
        direct[y] = product(square, signal[y], NN)
    finish(moving)
    y_in(2)
    finish(send_x(2))
    dual[...] = x_in(2) * (1.0 / z.count)
    mix(dual, True, None)
    x_out(3)
    moving = send_x(3)
    store(dual, dual_hbm)
    finish(moving)
    y_out(3)
    finish(send_y(3))
    for y in range(z.rows_y):
        put_cells(field_grad, y, depth_out(3, y) + direct[y])
    store(field_grad, grad_hbm)
    finish(stores)


def outer(z, block, spec, dual, first, second, grad, first_out, second_out, sems):
    part = pl.program_id(0)
    moves = [
        pltpu.make_async_copy(first, first_out, sems.at[0]),
        pltpu.make_async_copy(second, second_out, sems.at[1]),
    ]

    @pl.when((part == 0) & (pl.program_id(1) == 0))
    def _():
        for move in moves:
            move.start()

    sign = (1 - 2 * part).astype(jnp.float32)
    pairs = z.chan * z.chan
    for k in range(block):
        kx = pl.program_id(1) * block + k
        same = dual[pl.ds(part * z.chan * z.kp + kx, z.chan, stride=z.kp), :]
        cross = dual[pl.ds((1 - part) * z.chan * z.kp + kx, z.chan, stride=z.kp), :] * sign
        for c in range(z.chan):
            real = spec[pl.ds(c * z.kp + kx, 1), :]
            imag = spec[pl.ds((z.chan + c) * z.kp + kx, 1), :]
            at = k * pairs + c * z.chan
            grad[at : at + z.chan, 0, :] = real * same + imag * cross

    @pl.when((part == pl.num_programs(0) - 1) & (pl.program_id(1) == pl.num_programs(1) - 1))
    def _():
        for move in moves:
            move.wait()


def on_device(fields, cotangent, spectral, bypass):
    z = Sizes(fields.shape, spectral.shape, lax.axis_size("gx"), lax.axis_size("gy"))
    f32 = jnp.float32

    def rows(value):
        shaped = value.reshape(z.chan, z.rows_x, z.rows_y, z.tiles, LANES)
        return shaped.transpose(0, 1, 3, 2, 4).reshape(-1, LANES)

    def unrows(value):
        shaped = value.reshape(z.chan, z.rows_x, z.tiles, z.rows_y, LANES)
        return shaped.transpose(0, 1, 3, 2, 4).reshape(fields.shape)

    weights = spectral.transpose(0, 3, 4, 5, 2, 1).reshape(-1, z.qb)
    spread = np.kron(np.eye(z.chan), np.ones((z.rows_x, 1))).astype(np.float32)
    same_x = np.kron(np.ones((z.chan, z.chan)), np.eye(z.rows_x)).astype(np.float32)
    x_cols = z.nx * 2 * z.cp
    hbm = pl.BlockSpec(memory_space=pltpu.HBM)
    any_space = pl.BlockSpec(memory_space=pl.ANY)
    grid_rows = z.cx * z.rows_y * z.tiles
    y_block = (4, z.ny, z.mb2, z.rows_y * z.cp)
    x_block = (4, z.nx, 2 * z.qbp, z.cp)
    output, field_grad, spec, dual = pl.pallas_call(
        functools.partial(chain, z),
        out_shape=(
            jax.ShapeDtypeStruct((grid_rows, LANES), f32),
            jax.ShapeDtypeStruct((grid_rows, LANES), f32),
            jax.ShapeDtypeStruct((z.spec_rows, z.qb), f32),
            jax.ShapeDtypeStruct((z.spec_rows, z.qb), f32),
        ),
        in_specs=[hbm] * 8,
        out_specs=[hbm] * 4,
        scratch_shapes=[
            pltpu.VMEM((grid_rows, LANES), f32),
            pltpu.VMEM((grid_rows, LANES), f32),
            pltpu.VMEM((z.spec_rows, z.qb), f32),
            pltpu.VMEM((z.spec_rows, z.qb), f32),
            pltpu.VMEM((grid_rows, LANES), f32),
            pltpu.VMEM((grid_rows, LANES), f32),
            pltpu.VMEM((z.ny * z.mb2, z.cells), f32),
            pltpu.VMEM(bypass.shape, f32),
            pltpu.VMEM(spread.shape, f32),
            pltpu.VMEM(same_x.shape, f32),
            pltpu.VMEM(weights.shape, f32),
            pltpu.VMEM((z.spec_rows, x_cols), f32),
            pltpu.VMEM((z.ly, z.mb2, z.cp), f32),
            pltpu.VMEM((z.spec_rows, z.qb), f32),
            pltpu.VMEM((z.rows_y, z.cx, z.cells), f32),
            pltpu.VMEM((z.rows_y, z.cx, z.cells), f32),
            pltpu.VMEM(y_block, f32),
            pltpu.VMEM(y_block, f32),
            pltpu.VMEM(x_block, f32),
            pltpu.VMEM(x_block, f32),
            pltpu.SemaphoreType.DMA((4, z.ny)),
            pltpu.SemaphoreType.DMA((4, z.ny)),
            pltpu.SemaphoreType.DMA((4, z.nx)),
            pltpu.SemaphoreType.DMA((4, z.nx)),
            pltpu.SemaphoreType.DMA((8,)),
            pltpu.SemaphoreType.DMA((4,)),
        ],
        compiler_params=pltpu.CompilerParams(
            collective_id=0, has_side_effects=True, vmem_limit_bytes=61 << 20
        ),
        name="fourier_chain",
    )(
        rows(fields), rows(cotangent), depth_table(z), bypass, spread, same_x, weights, x_table(z)
    )
    block = 4 if z.kx % 4 == 0 else z.kx
    per_step = block * z.chan * z.chan
    local_grad, output, field_grad = pl.pallas_call(
        functools.partial(outer, z, block),
        grid=(2, z.kx // block),
        out_shape=(
            jax.ShapeDtypeStruct((weights.shape[0], 1, z.qb), f32),
            jax.ShapeDtypeStruct((grid_rows, LANES), f32),
            jax.ShapeDtypeStruct((grid_rows, LANES), f32),
        ),
        in_specs=[pl.BlockSpec((z.spec_rows, z.qb), lambda p, k: (0, 0))] * 2 + [any_space] * 2,
        out_specs=(
            pl.BlockSpec((per_step, 1, z.qb), lambda p, k: (p * (z.kx // block) + k, 0, 0)),
            any_space,
            any_space,
        ),
        scratch_shapes=[pltpu.SemaphoreType.DMA((2,))],
        compiler_params=pltpu.CompilerParams(vmem_limit_bytes=61 << 20),
        name="outer_products",
    )(spec, dual, output, field_grad)
    spectral_grad = local_grad.reshape(2, z.kx, z.chan, z.chan, 1, z.qb).transpose(0, 5, 4, 1, 2, 3)
    if lax.axis_size("dp") > 1:
        spectral_grad = lax.psum(spectral_grad, "dp")
    return (unrows(output), unrows(field_grad), spectral_grad)


def solution(mesh):
    cells = P("dp", None, "gx", "gy", None)
    weights = P(None, "gx", "gy", None, None, None)
    return jax.shard_map(
        on_device,
        mesh=mesh,
        in_specs=(cells, cells, weights, P()),
        out_specs=(cells, cells, weights),
        check_vma=False,
    )
```

```python
import functools
import math

import jax
import jax.numpy as jnp
import numpy as np
from jax import lax
from jax.experimental import pallas as pl
from jax.experimental.pallas import tpu as pltpu
from jax.sharding import PartitionSpec as P

STEPS = 8
MODES_X = 12
MODES_Y = 12
MODES_Z = 12
MODES_T = 8
LANES = 128
MESH = pl.DeviceIdType.MESH
close = lax.Precision.HIGH
NN = (((1,), (0,)), ((), ()))
NT = (((1,), (1,)), ((), ()))
TN = (((0,), (0,)), ((), ()))


def up(value, step):
    return -(-value // step) * step


def product(left, right, dims):
    return lax.dot_general(left, right, dims, precision=close, preferred_element_type=jnp.float32)


def signed(amount):
    ids = np.arange(amount)
    return np.where(ids < amount // 2, ids, ids - amount)


class Sizes:
    def __init__(self, sample, spectral, size_x, size_y):
        _, self.chan, self.rows_x, self.rows_y, self.cells = sample
        self.nx, self.ny = size_x, size_y
        self.full_x, self.full_y = self.rows_x * size_x, self.rows_y * size_y
        self.count = self.full_x * self.full_y * self.cells
        self.tiles = self.cells // LANES
        self.qb = spectral[1]
        self.kx = spectral[3]
        self.mb = MODES_Z * MODES_T // size_y
        self.ly = MODES_Y
        self.mb2 = up(2 * self.mb, 8)
        self.half = self.mb2 // 2
        self.cx = self.chan * self.rows_x
        self.cp = up(self.cx, LANES)
        self.kp = up(self.kx, 8)
        self.qbp = up(self.qb, 8)
        self.spec_rows = 2 * self.chan * self.kp

    def pieces(self, mode):
        start, stop, found = mode * self.mb, (mode + 1) * self.mb, []
        while start < stop:
            owner = start // self.qb
            rows = min(stop, (owner + 1) * self.qb) - start
            found.append((owner, start - owner * self.qb, start - mode * self.mb, rows))
            start += rows
        return found


def depth_table(z):
    depth = z.cells // STEPS
    modes = np.arange(MODES_Z * MODES_T)
    freq_z, freq_t = signed(MODES_Z)[modes // MODES_T], signed(MODES_T)[modes % MODES_T]
    cell = np.arange(z.cells)
    turns = freq_z[:, None] * (cell // STEPS) * STEPS + freq_t[:, None] * (cell % STEPS) * depth
    angle = (turns % z.cells) * (2.0 * math.pi / z.cells)
    table = np.zeros((z.ny, 2, z.half, z.cells))
    table[:, 0, : z.mb] = np.cos(angle).reshape(z.ny, z.mb, z.cells)
    table[:, 1, : z.mb] = -np.sin(angle).reshape(z.ny, z.mb, z.cells)
    return table.reshape(z.ny * z.mb2, z.cells).astype(np.float32)


def x_table(z):
    angle = (signed(z.kx)[:, None] * np.arange(z.full_x) % z.full_x) * (2.0 * math.pi / z.full_x)
    cosine = np.cos(angle).reshape(z.kx, z.nx, z.rows_x)
    sine = np.sin(angle).reshape(z.kx, z.nx, z.rows_x)
    table = np.zeros((2, z.chan, z.kp, z.nx, 2, z.cp))
    for c in range(z.chan):
        cols = slice(c * z.rows_x, (c + 1) * z.rows_x)
        table[0, c, : z.kx, :, 0, cols] = cosine
        table[0, c, : z.kx, :, 1, cols] = sine
        table[1, c, : z.kx, :, 0, cols] = -sine
        table[1, c, : z.kx, :, 1, cols] = cosine
    return table.reshape(z.spec_rows, z.nx * 2 * z.cp).astype(np.float32)


def chain(
    z, fields_hbm, cotangent_hbm, depth_hbm, bypass_hbm, spread_hbm, same_hbm, w_hbm, x_hbm,
    output_hbm, grad_hbm, spec_hbm, dual_hbm,
    output, field_grad, spec, dual, fields, cotangent, depth, bypass, spread, same_x, w, xt, unit, mixed, signal, direct, sg, rg, sx, rx, gs, gr, xs, xr, load_sems, store_sems,
):
    me_x, me_y = lax.axis_index("gx"), lax.axis_index("gy")
    axes = {"gx": (me_x, z.nx), "gy": (me_y, z.ny)}

    barrier = pltpu.get_barrier_semaphore()
    for axis, (me, n) in axes.items():
        for step in range(1, n):
            pl.semaphore_signal(
                barrier, inc=1, device_id={axis: lax.rem(me + step, n)}, device_id_type=MESH
            )
    loads = {}
    for name, src, dst in (
        ("depth", depth_hbm, depth),
        ("fields", fields_hbm, fields),
        ("bypass", bypass_hbm, bypass),
        ("spread", spread_hbm, spread),
        ("same_x", same_hbm, same_x),
        ("x", x_hbm, xt),
        ("w", w_hbm, w),
        ("cotangent", cotangent_hbm, cotangent),
    ):
        loads[name] = pltpu.make_async_copy(src, dst, load_sems.at[len(loads)])
        loads[name].start()

    stores = []

    def store(src, dst):
        stores.append(pltpu.make_async_copy(src, dst, store_sems.at[len(stores)]))
        stores[-1].start()

    def send(axis, src, dst, send_sem, recv_sem):
        me, n = axes[axis]
        copies = []
        for step in range(1, n):
            peer = lax.rem(me + step, n)
            copy = pltpu.make_async_remote_copy(
                src_ref=src.at[peer],
                dst_ref=dst.at[me],
                send_sem=send_sem.at[step],
                recv_sem=recv_sem.at[step],
                device_id={axis: peer},
                device_id_type=MESH,
            )
            copy.start()
            copies.append(copy)
        dst[me] = src[me]
        return copies

    def send_y(turn):
        return send("gy", sg.at[turn], rg.at[turn], gs.at[turn], gr.at[turn])

    def send_x(turn):
        return send("gx", sx.at[turn], rx.at[turn], xs.at[turn], xr.at[turn])

    def finish(copies):
        for copy in copies:
            copy.wait()

    stride = z.tiles * z.rows_y

    def cells_of(ref, y):
        parts = [ref[pl.ds(t * z.rows_y + y, z.cx, stride=stride), :] for t in range(z.tiles)]
        return jnp.concatenate(parts, axis=1)

    def put_cells(ref, y, value):
        for t in range(z.tiles):
            ref[pl.ds(t * z.rows_y + y, z.cx, stride=stride), :] = value[:, t * LANES : (t + 1) * LANES]

    def lanes(y):
        return slice((y % z.rows_y) * z.cp, (y % z.rows_y + 1) * z.cp)

    def depth_in(turn, y, cells):
        if z.cp > z.cx:
            cells = jnp.concatenate([cells, jnp.zeros((z.cp - z.cx, z.cells), jnp.float32)], axis=0)
        found = product(depth[...], cells, NT)
        for block in range(z.ny):
            sg[turn, block, :, lanes(y)] = found[block * z.mb2 : (block + 1) * z.mb2]

    def depth_out(turn, y):
        held = rg[turn, :, :, lanes(y)].reshape(z.ny * z.mb2, z.cp)
        return product(held, depth[...], TN)[: z.cx]

    first_half = lax.broadcasted_iota(jnp.int32, (z.mb2, z.cp), 0) < z.half
    minus_i = jnp.where(first_half, 1.0, -1.0)

    def times_minus_i(value):
        return pltpu.roll(value, z.half, 0) * minus_i

    def wave(y, f):
        angle = 2.0 * math.pi * ((y * f) % z.full_y) / z.full_y
        return math.cos(angle), math.sin(angle)

    def total(terms):
        out = None
        for factor, value in terms:
            if abs(factor) < 1e-12:
                continue
            term = value if factor == 1.0 else value * factor
            out = term if out is None else out + term
        return out

    mid, top = z.full_y // 2, z.ly // 2

    def y_in(turn):
        at = [rg[turn, y // z.rows_y, :, lanes(y)] for y in range(z.full_y)]
        even = [at[y] if y in (0, mid) else at[y] + at[z.full_y - y] for y in range(mid + 1)]
        odd = [None if y in (0, mid) else at[y] - at[z.full_y - y] for y in range(mid)]

        def put(mode, value):
            for part in range(2):
                for owner, there, here, rows in z.pieces(mode):
                    low, base = part * z.half + here, part * z.qbp + there
                    sx[turn, owner, base : base + rows, :] = value[low : low + rows]

        for f in range(top + 1):
            cosines = total([(wave(y, f)[0], even[y]) for y in range(mid + 1)])
            if f == 0:
                put(0, cosines)
                continue
            sines = times_minus_i(total([(wave(y, f)[1], odd[y]) for y in range(1, mid)]))
            if f < top:
                put(f, cosines + sines)
            put(z.ly - f, cosines - sines)

    def y_out(turn):
        for mode in range(z.ly):
            for part in range(2):
                for owner, there, here, rows in z.pieces(mode):
                    low, base = part * z.half + here, part * z.qbp + there
                    unit[mode, low : low + rows, :] = rx[turn, owner, base : base + rows, :]
        even, odd = [unit[0]], [None]
        for f in range(1, top + 1):
            back = unit[z.ly - f]
            ahead = unit[f] if f < top else None
            even.append(back if ahead is None else ahead + back)
            odd.append(times_minus_i(back if ahead is None else back - ahead))
        for y in range(mid + 1):
            cosines = total([(wave(y, f)[0], even[f]) for f in range(top + 1)])
            sines = total([(wave(y, f)[1], odd[f]) for f in range(1, top + 1)]) if 0 < y < mid else None
            if sines is None:
                sg[turn, y // z.rows_y, :, lanes(y)] = cosines
                continue
            other = z.full_y - y
            sg[turn, y // z.rows_y, :, lanes(y)] = cosines + sines
            sg[turn, other // z.rows_y, :, lanes(other)] = cosines - sines

    def x_in(turn):
        held = [
            rx[turn, s, part * z.qbp : part * z.qbp + z.qb, :]
            for s in range(z.nx)
            for part in range(2)
        ]
        return product(xt[...], jnp.concatenate(held, axis=1), NT)

    def x_out(turn):
        found = product(mixed[...], xt[...], TN)
        for s in range(z.nx):
            for part in range(2):
                col = (2 * s + part) * z.cp
                sx[turn, s, part * z.qbp : part * z.qbp + z.qb, :] = found[:, col : col + z.cp]

    pairs = z.chan * z.chan

    def weight(part, row):
        return w[pl.ds(part * z.kx * pairs + row, z.kx, stride=pairs), :]

    def modes(ref, part, channel):
        return ref[pl.ds(pl.multiple_of((part * z.chan + channel) * z.kp, 8), z.kx), :]

    def mix(source, adjoint, scale):
        sign = -1.0 if adjoint else 1.0

        def body(to, carry):
            real = jnp.zeros((z.kx, z.qb), jnp.float32)
            imag = jnp.zeros((z.kx, z.qb), jnp.float32)
            for c in range(z.chan):
                row = to * z.chan + c if adjoint else c * z.chan + to
                w_real, w_imag = weight(0, row), weight(1, row)
                s_real, s_imag = modes(source, 0, c), modes(source, 1, c)
                real = real + s_real * w_real - sign * (s_imag * w_imag)
                imag = imag + s_imag * w_real + sign * (s_real * w_imag)
            for part, value in ((0, real), (1, imag)):
                at = pl.multiple_of((part * z.chan + to) * z.kp, 8)
                mixed[pl.ds(at, z.kx), :] = value if scale is None else value * scale
            return carry

        lax.fori_loop(0, z.chan, body, 0)

    loads["depth"].wait()
    loads["fields"].wait()
    for y in range(z.rows_y):
        depth_in(0, y, cells_of(fields, y))
    pl.semaphore_wait(barrier, z.nx + z.ny - 2)
    moving = send_y(0)
    mixed[...] = jnp.zeros_like(mixed)
    if z.half != z.mb:
        unit[...] = jnp.zeros_like(unit)
    for name in ("bypass", "spread", "same_x"):
        loads[name].wait()
    exact = lax.Precision.HIGHEST
    wide = lax.dot_general(spread[...], bypass[...], NN, precision=exact)
    square = lax.dot_general(wide, spread[...], NT, precision=exact) * same_x[...]
    for y in range(z.rows_y):
        direct[y] = product(square, cells_of(fields, y), TN)
    finish(moving)
    y_in(0)
    moving = send_x(0)
    loads["x"].wait()
    finish(moving)
    spec[...] = x_in(0)
    loads["w"].wait()
    mix(spec, False, 1.0 / z.count)
    x_out(1)
    finish(send_x(1))
    y_out(1)
    finish(send_y(1))
    loads["cotangent"].wait()

    root = math.sqrt(2.0 / math.pi)
    for y in range(z.rows_y):
        pre = depth_out(1, y) + direct[y]
        square_pre = pre * pre
        bend = jnp.tanh(root * (pre + 0.044715 * (square_pre * pre)))
        put_cells(output, y, 0.5 * pre * (1.0 + bend))
        slope = 0.5 * (1.0 + bend) + 0.5 * pre * (1.0 - bend * bend) * (
            root * (1.0 + 3.0 * 0.044715 * square_pre)
        )
        back = cells_of(cotangent, y) * slope
        signal[y] = back
        depth_in(2, y, back)

    moving = send_y(2)
    store(spec, spec_hbm)
    store(output, output_hbm)
    for y in range(z.rows_y):
        direct[y] = product(square, signal[y], NN)
    finish(moving)
    y_in(2)
    finish(send_x(2))
    dual[...] = x_in(2) * (1.0 / z.count)
    mix(dual, True, None)
    x_out(3)
    moving = send_x(3)
    store(dual, dual_hbm)
    finish(moving)
    y_out(3)
    finish(send_y(3))
    for y in range(z.rows_y):
        put_cells(field_grad, y, depth_out(3, y) + direct[y])
    store(field_grad, grad_hbm)
    finish(stores)


def outer(z, spec, dual, first, second, grad_hbm, first_out, second_out, grad, sems):
    pairs = z.chan * z.chan
    per_part = z.kx * pairs
    moves = [
        pltpu.make_async_copy(first, first_out, sems.at[0]),
        pltpu.make_async_copy(second, second_out, sems.at[1]),
    ]
    for move in moves:
        move.start()
    for part in range(2):
        sign = 1.0 - 2.0 * part

        def body(kx, carry):
            same = dual[pl.ds(part * z.chan * z.kp + kx, z.chan, stride=z.kp), :]
            cross = dual[pl.ds((1 - part) * z.chan * z.kp + kx, z.chan, stride=z.kp), :] * sign
            for c in range(z.chan):
                real = spec[pl.ds(c * z.kp + kx, 1), :]
                imag = spec[pl.ds((z.chan + c) * z.kp + kx, 1), :]
                at = part * per_part + kx * pairs + c * z.chan
                grad[pl.ds(at, z.chan), :] = real * same + imag * cross
            return carry

        lax.fori_loop(0, z.kx, body, 0)
        rows = pl.ds(part * per_part, per_part)
        move = pltpu.make_async_copy(grad.at[rows], grad_hbm.at[rows, 0], sems.at[2 + part])
        move.start()
        moves.append(move)
    for move in moves:
        move.wait()


def on_device(fields, cotangent, spectral, bypass):
    z = Sizes(fields.shape, spectral.shape, lax.axis_size("gx"), lax.axis_size("gy"))
    f32 = jnp.float32

    def rows(value):
        shaped = value.reshape(z.chan, z.rows_x, z.rows_y, z.tiles, LANES)
        return shaped.transpose(0, 1, 3, 2, 4).reshape(-1, LANES)

    def unrows(value):
        shaped = value.reshape(z.chan, z.rows_x, z.tiles, z.rows_y, LANES)
        return shaped.transpose(0, 1, 3, 2, 4).reshape(fields.shape)

    weights = spectral.transpose(0, 3, 4, 5, 2, 1).reshape(-1, z.qb)
    spread = np.kron(np.eye(z.chan), np.ones((z.rows_x, 1))).astype(np.float32)
    same_x = np.kron(np.ones((z.chan, z.chan)), np.eye(z.rows_x)).astype(np.float32)
    x_cols = z.nx * 2 * z.cp
    vmem = pl.BlockSpec(memory_space=pltpu.VMEM)
    hbm = pl.BlockSpec(memory_space=pltpu.HBM)
    any_space = pl.BlockSpec(memory_space=pl.ANY)
    grid_rows = z.cx * z.rows_y * z.tiles
    y_block = (4, z.ny, z.mb2, z.rows_y * z.cp)
    x_block = (4, z.nx, 2 * z.qbp, z.cp)
    output, field_grad, spec, dual = pl.pallas_call(
        functools.partial(chain, z),
        out_shape=(
            jax.ShapeDtypeStruct((grid_rows, LANES), f32),
            jax.ShapeDtypeStruct((grid_rows, LANES), f32),
            jax.ShapeDtypeStruct((z.spec_rows, z.qb), f32),
            jax.ShapeDtypeStruct((z.spec_rows, z.qb), f32),
        ),
        in_specs=[hbm] * 8,
        out_specs=[hbm] * 4,
        scratch_shapes=[
            pltpu.VMEM((grid_rows, LANES), f32),
            pltpu.VMEM((grid_rows, LANES), f32),
            pltpu.VMEM((z.spec_rows, z.qb), f32),
            pltpu.VMEM((z.spec_rows, z.qb), f32),
            pltpu.VMEM((grid_rows, LANES), f32),
            pltpu.VMEM((grid_rows, LANES), f32),
            pltpu.VMEM((z.ny * z.mb2, z.cells), f32),
            pltpu.VMEM(bypass.shape, f32),
            pltpu.VMEM(spread.shape, f32),
            pltpu.VMEM(same_x.shape, f32),
            pltpu.VMEM(weights.shape, f32),
            pltpu.VMEM((z.spec_rows, x_cols), f32),
            pltpu.VMEM((z.ly, z.mb2, z.cp), f32),
            pltpu.VMEM((z.spec_rows, z.qb), f32),
            pltpu.VMEM((z.rows_y, z.cx, z.cells), f32),
            pltpu.VMEM((z.rows_y, z.cx, z.cells), f32),
            pltpu.VMEM(y_block, f32),
            pltpu.VMEM(y_block, f32),
            pltpu.VMEM(x_block, f32),
            pltpu.VMEM(x_block, f32),
            pltpu.SemaphoreType.DMA((4, z.ny)),
            pltpu.SemaphoreType.DMA((4, z.ny)),
            pltpu.SemaphoreType.DMA((4, z.nx)),
            pltpu.SemaphoreType.DMA((4, z.nx)),
            pltpu.SemaphoreType.DMA((8,)),
            pltpu.SemaphoreType.DMA((4,)),
        ],
        compiler_params=pltpu.CompilerParams(
            collective_id=0, has_side_effects=True, vmem_limit_bytes=61 << 20
        ),
        name="fourier_chain",
    )(
        rows(fields), rows(cotangent), depth_table(z), bypass, spread, same_x, weights, x_table(z)
    )
    local_grad, output, field_grad = pl.pallas_call(
        functools.partial(outer, z),
        out_shape=(
            jax.ShapeDtypeStruct((weights.shape[0], 1, z.qb), f32),
            jax.ShapeDtypeStruct((grid_rows, LANES), f32),
            jax.ShapeDtypeStruct((grid_rows, LANES), f32),
        ),
        in_specs=[vmem] * 2 + [any_space] * 2,
        out_specs=[any_space] * 3,
        scratch_shapes=[pltpu.VMEM(weights.shape, f32), pltpu.SemaphoreType.DMA((4,))],
        compiler_params=pltpu.CompilerParams(vmem_limit_bytes=61 << 20),
        name="outer_products",
    )(spec, dual, output, field_grad)
    spectral_grad = local_grad.reshape(2, z.kx, z.chan, z.chan, 1, z.qb).transpose(0, 5, 4, 1, 2, 3)
    if lax.axis_size("dp") > 1:
        spectral_grad = lax.psum(spectral_grad, "dp")
    return (unrows(output), unrows(field_grad), spectral_grad)


def solution(mesh):
    cells = P("dp", None, "gx", "gy", None)
    weights = P(None, "gx", "gy", None, None, None)
    return jax.shard_map(
        on_device,
        mesh=mesh,
        in_specs=(cells, cells, weights, P()),
        out_specs=(cells, cells, weights),
        check_vma=False,
    )
```

```python
import functools
import math

import jax
import jax.numpy as jnp
import numpy as np
from jax import lax
from jax.experimental import pallas as pl
from jax.experimental.pallas import tpu as pltpu
from jax.sharding import PartitionSpec as P

STEPS = 8
MODES_X = 12
MODES_Y = 12
MODES_Z = 12
MODES_T = 8
LANES = 128
MESH = pl.DeviceIdType.MESH
close = lax.Precision.HIGH
NN = (((1,), (0,)), ((), ()))
NT = (((1,), (1,)), ((), ()))
TN = (((0,), (0,)), ((), ()))


def up(value, step):
    return -(-value // step) * step


def product(left, right, dims):
    return lax.dot_general(left, right, dims, precision=close, preferred_element_type=jnp.float32)


def signed(amount):
    ids = np.arange(amount)
    return np.where(ids < amount // 2, ids, ids - amount)


class Sizes:
    def __init__(self, sample, spectral, size_x, size_y):
        _, self.chan, self.rows_x, self.rows_y, self.cells = sample
        self.nx, self.ny = size_x, size_y
        self.full_x, self.full_y = self.rows_x * size_x, self.rows_y * size_y
        self.count = self.full_x * self.full_y * self.cells
        self.tiles = self.cells // LANES
        self.qb = spectral[1]
        self.kx = spectral[3]
        self.mb = MODES_Z * MODES_T // size_y
        self.ly = MODES_Y
        self.mb2 = up(2 * self.mb, 8)
        self.half = self.mb2 // 2
        self.cx = self.chan * self.rows_x
        self.cp = up(self.cx, LANES)
        self.kp = up(self.kx, 8)
        self.qbp = up(self.qb, 8)
        self.spec_rows = 2 * self.chan * self.kp

    def pieces(self, mode):
        start, stop, found = mode * self.mb, (mode + 1) * self.mb, []
        while start < stop:
            owner = start // self.qb
            rows = min(stop, (owner + 1) * self.qb) - start
            found.append((owner, start - owner * self.qb, start - mode * self.mb, rows))
            start += rows
        return found


def depth_table(z):
    depth = z.cells // STEPS
    modes = np.arange(MODES_Z * MODES_T)
    freq_z, freq_t = signed(MODES_Z)[modes // MODES_T], signed(MODES_T)[modes % MODES_T]
    cell = np.arange(z.cells)
    turns = freq_z[:, None] * (cell // STEPS) * STEPS + freq_t[:, None] * (cell % STEPS) * depth
    angle = (turns % z.cells) * (2.0 * math.pi / z.cells)
    table = np.zeros((z.ny, 2, z.half, z.cells))
    table[:, 0, : z.mb] = np.cos(angle).reshape(z.ny, z.mb, z.cells)
    table[:, 1, : z.mb] = -np.sin(angle).reshape(z.ny, z.mb, z.cells)
    return table.reshape(z.ny * z.mb2, z.cells).astype(np.float32)


def x_table(z):
    angle = (signed(z.kx)[:, None] * np.arange(z.full_x) % z.full_x) * (2.0 * math.pi / z.full_x)
    cosine = np.cos(angle).reshape(z.kx, z.nx, z.rows_x)
    sine = np.sin(angle).reshape(z.kx, z.nx, z.rows_x)
    table = np.zeros((2, z.chan, z.kp, z.nx, 2, z.cp))
    for c in range(z.chan):
        cols = slice(c * z.rows_x, (c + 1) * z.rows_x)
        table[0, c, : z.kx, :, 0, cols] = cosine
        table[0, c, : z.kx, :, 1, cols] = sine
        table[1, c, : z.kx, :, 0, cols] = -sine
        table[1, c, : z.kx, :, 1, cols] = cosine
    return table.reshape(z.spec_rows, z.nx * 2 * z.cp).astype(np.float32)


def chain(
    z, fields_hbm, cotangent_hbm, depth_hbm, bypass_hbm, spread_hbm, same_hbm, w_hbm, x_hbm,
    output_hbm, grad_hbm, spec_hbm, dual_hbm,
    output, field_grad, spec, dual, fields, cotangent, depth, bypass, spread, same_x, w, xt, unit, mixed, signal, direct, sg, rg, sx, rx, gs, gr, xs, xr, load_sems, store_sems,
):
    me_x, me_y = lax.axis_index("gx"), lax.axis_index("gy")
    axes = {"gx": (me_x, z.nx), "gy": (me_y, z.ny)}

    barrier = pltpu.get_barrier_semaphore()
    for axis, (me, n) in axes.items():
        for step in range(1, n):
            pl.semaphore_signal(
                barrier, inc=1, device_id={axis: lax.rem(me + step, n)}, device_id_type=MESH
            )
    loads = {}
    for name, src, dst in (
        ("depth", depth_hbm, depth),
        ("fields", fields_hbm, fields),
        ("bypass", bypass_hbm, bypass),
        ("spread", spread_hbm, spread),
        ("same_x", same_hbm, same_x),
        ("x", x_hbm, xt),
        ("w", w_hbm, w),
        ("cotangent", cotangent_hbm, cotangent),
    ):
        loads[name] = pltpu.make_async_copy(src, dst, load_sems.at[len(loads)])
        loads[name].start()

    stores = []

    def store(src, dst):
        stores.append(pltpu.make_async_copy(src, dst, store_sems.at[len(stores)]))
        stores[-1].start()

    def send(axis, src, dst, send_sem, recv_sem):
        me, n = axes[axis]
        copies = []
        for step in range(1, n):
            peer = lax.rem(me + step, n)
            copy = pltpu.make_async_remote_copy(
                src_ref=src.at[peer],
                dst_ref=dst.at[me],
                send_sem=send_sem.at[step],
                recv_sem=recv_sem.at[step],
                device_id={axis: peer},
                device_id_type=MESH,
            )
            copy.start()
            copies.append(copy)
        dst[me] = src[me]
        return copies

    def send_y(turn):
        return send("gy", sg.at[turn], rg.at[turn], gs.at[turn], gr.at[turn])

    def send_x(turn):
        return send("gx", sx.at[turn], rx.at[turn], xs.at[turn], xr.at[turn])

    def finish(copies):
        for copy in copies:
            copy.wait()

    stride = z.tiles * z.rows_y

    def cells_of(ref, y):
        parts = [ref[pl.ds(t * z.rows_y + y, z.cx, stride=stride), :] for t in range(z.tiles)]
        return jnp.concatenate(parts, axis=1)

    def put_cells(ref, y, value):
        for t in range(z.tiles):
            ref[pl.ds(t * z.rows_y + y, z.cx, stride=stride), :] = value[:, t * LANES : (t + 1) * LANES]

    def lanes(y):
        return slice((y % z.rows_y) * z.cp, (y % z.rows_y + 1) * z.cp)

    def depth_in(turn, y, cells):
        if z.cp > z.cx:
            cells = jnp.concatenate([cells, jnp.zeros((z.cp - z.cx, z.cells), jnp.float32)], axis=0)
        found = product(depth[...], cells, NT)
        for block in range(z.ny):
            sg[turn, block, :, lanes(y)] = found[block * z.mb2 : (block + 1) * z.mb2]

    def depth_out(turn, y):
        held = rg[turn, :, :, lanes(y)].reshape(z.ny * z.mb2, z.cp)
        return product(held, depth[...], TN)[: z.cx]

    first_half = lax.broadcasted_iota(jnp.int32, (z.mb2, z.cp), 0) < z.half
    minus_i = jnp.where(first_half, 1.0, -1.0)

    def times_minus_i(value):
        return pltpu.roll(value, z.half, 0) * minus_i

    def wave(y, f):
        angle = 2.0 * math.pi * ((y * f) % z.full_y) / z.full_y
        return math.cos(angle), math.sin(angle)

    def total(terms):
        out = None
        for factor, value in terms:
            if abs(factor) < 1e-12:
                continue
            term = value if factor == 1.0 else value * factor
            out = term if out is None else out + term
        return out

    mid, top = z.full_y // 2, z.ly // 2

    def y_in(turn):
        at = [rg[turn, y // z.rows_y, :, lanes(y)] for y in range(z.full_y)]
        even = [at[y] if y in (0, mid) else at[y] + at[z.full_y - y] for y in range(mid + 1)]
        odd = [None if y in (0, mid) else at[y] - at[z.full_y - y] for y in range(mid)]

        def put(mode, value):
            for part in range(2):
                for owner, there, here, rows in z.pieces(mode):
                    low, base = part * z.half + here, part * z.qbp + there
                    sx[turn, owner, base : base + rows, :] = value[low : low + rows]

        for f in range(top + 1):
            cosines = total([(wave(y, f)[0], even[y]) for y in range(mid + 1)])
            if f == 0:
                put(0, cosines)
                continue
            sines = times_minus_i(total([(wave(y, f)[1], odd[y]) for y in range(1, mid)]))
            if f < top:
                put(f, cosines + sines)
            put(z.ly - f, cosines - sines)

    def y_out(turn):
        for mode in range(z.ly):
            for part in range(2):
                for owner, there, here, rows in z.pieces(mode):
                    low, base = part * z.half + here, part * z.qbp + there
                    unit[mode, low : low + rows, :] = rx[turn, owner, base : base + rows, :]
        even, odd = [unit[0]], [None]
        for f in range(1, top + 1):
            back = unit[z.ly - f]
            ahead = unit[f] if f < top else None
            even.append(back if ahead is None else ahead + back)
            odd.append(times_minus_i(back if ahead is None else back - ahead))
        for y in range(mid + 1):
            cosines = total([(wave(y, f)[0], even[f]) for f in range(top + 1)])
            sines = total([(wave(y, f)[1], odd[f]) for f in range(1, top + 1)]) if 0 < y < mid else None
            if sines is None:
                sg[turn, y // z.rows_y, :, lanes(y)] = cosines
                continue
            other = z.full_y - y
            sg[turn, y // z.rows_y, :, lanes(y)] = cosines + sines
            sg[turn, other // z.rows_y, :, lanes(other)] = cosines - sines

    def x_in(turn):
        held = [
            rx[turn, s, part * z.qbp : part * z.qbp + z.qb, :]
            for s in range(z.nx)
            for part in range(2)
        ]
        return product(xt[...], jnp.concatenate(held, axis=1), NT)

    def x_out(turn):
        found = product(mixed[...], xt[...], TN)
        for s in range(z.nx):
            for part in range(2):
                col = (2 * s + part) * z.cp
                sx[turn, s, part * z.qbp : part * z.qbp + z.qb, :] = found[:, col : col + z.cp]

    pairs = z.chan * z.chan

    def weight(part, row):
        return w[pl.ds(part * z.kx * pairs + row, z.kx, stride=pairs), :][:, : z.qb]

    def modes(ref, part, channel):
        return ref[pl.ds(pl.multiple_of((part * z.chan + channel) * z.kp, 8), z.kx), :]

    def mix(source, adjoint, scale):
        sign = -1.0 if adjoint else 1.0

        def body(to, carry):
            real = jnp.zeros((z.kx, z.qb), jnp.float32)
            imag = jnp.zeros((z.kx, z.qb), jnp.float32)
            for c in range(z.chan):
                row = to * z.chan + c if adjoint else c * z.chan + to
                w_real, w_imag = weight(0, row), weight(1, row)
                s_real, s_imag = modes(source, 0, c), modes(source, 1, c)
                real = real + s_real * w_real - sign * (s_imag * w_imag)
                imag = imag + s_imag * w_real + sign * (s_real * w_imag)
            for part, value in ((0, real), (1, imag)):
                at = pl.multiple_of((part * z.chan + to) * z.kp, 8)
                mixed[pl.ds(at, z.kx), :] = value if scale is None else value * scale
            return carry

        lax.fori_loop(0, z.chan, body, 0)

    loads["depth"].wait()
    loads["fields"].wait()
    for y in range(z.rows_y):
        depth_in(0, y, cells_of(fields, y))
    pl.semaphore_wait(barrier, z.nx + z.ny - 2)
    moving = send_y(0)
    mixed[...] = jnp.zeros_like(mixed)
    if z.half != z.mb:
        unit[...] = jnp.zeros_like(unit)
    for name in ("bypass", "spread", "same_x"):
        loads[name].wait()
    exact = lax.Precision.HIGHEST
    wide = lax.dot_general(spread[...], bypass[...], NN, precision=exact)
    square = lax.dot_general(wide, spread[...], NT, precision=exact) * same_x[...]
    for y in range(z.rows_y):
        direct[y] = product(square, cells_of(fields, y), TN)
    finish(moving)
    y_in(0)
    moving = send_x(0)
    loads["x"].wait()
    finish(moving)
    spec[...] = x_in(0)
    loads["w"].wait()
    mix(spec, False, 1.0 / z.count)
    x_out(1)
    finish(send_x(1))
    y_out(1)
    finish(send_y(1))
    loads["cotangent"].wait()

    root = math.sqrt(2.0 / math.pi)
    for y in range(z.rows_y):
        pre = depth_out(1, y) + direct[y]
        square_pre = pre * pre
        bend = jnp.tanh(root * (pre + 0.044715 * (square_pre * pre)))
        put_cells(output, y, 0.5 * pre * (1.0 + bend))
        slope = 0.5 * (1.0 + bend) + 0.5 * pre * (1.0 - bend * bend) * (
            root * (1.0 + 3.0 * 0.044715 * square_pre)
        )
        back = cells_of(cotangent, y) * slope
        signal[y] = back
        depth_in(2, y, back)

    moving = send_y(2)
    store(spec, spec_hbm)
    store(output, output_hbm)
    for y in range(z.rows_y):
        direct[y] = product(square, signal[y], NN)
    finish(moving)
    y_in(2)
    finish(send_x(2))
    dual[...] = x_in(2) * (1.0 / z.count)
    mix(dual, True, None)
    x_out(3)
    moving = send_x(3)
    store(dual, dual_hbm)
    finish(moving)
    y_out(3)
    finish(send_y(3))
    for y in range(z.rows_y):
        put_cells(field_grad, y, depth_out(3, y) + direct[y])
    store(field_grad, grad_hbm)
    finish(stores)


def outer(z, spec, dual, first, second, grad_hbm, first_out, second_out, grad, sems):
    pairs = z.chan * z.chan
    per_part = z.kx * pairs
    moves = [
        pltpu.make_async_copy(first, first_out, sems.at[0]),
        pltpu.make_async_copy(second, second_out, sems.at[1]),
    ]
    for move in moves:
        move.start()
    for part in range(2):
        sign = 1.0 - 2.0 * part

        def body(kx, carry):
            same = dual[pl.ds(part * z.chan * z.kp + kx, z.chan, stride=z.kp), :]
            cross = dual[pl.ds((1 - part) * z.chan * z.kp + kx, z.chan, stride=z.kp), :] * sign
            for c in range(z.chan):
                real = spec[pl.ds(c * z.kp + kx, 1), :]
                imag = spec[pl.ds((z.chan + c) * z.kp + kx, 1), :]
                at = part * per_part + kx * pairs + c * z.chan
                grad[pl.ds(at, z.chan), : z.qb] = real * same + imag * cross
            return carry

        lax.fori_loop(0, z.kx, body, 0)
        rows = pl.ds(part * per_part, per_part)
        move = pltpu.make_async_copy(grad.at[rows], grad_hbm.at[rows], sems.at[2 + part])
        move.start()
        moves.append(move)
    for move in moves:
        move.wait()


def on_device(fields, cotangent, spectral, bypass):
    z = Sizes(fields.shape, spectral.shape, lax.axis_size("gx"), lax.axis_size("gy"))
    f32 = jnp.float32

    def rows(value):
        shaped = value.reshape(z.chan, z.rows_x, z.rows_y, z.tiles, LANES)
        return shaped.transpose(0, 1, 3, 2, 4).reshape(-1, LANES)

    def unrows(value):
        shaped = value.reshape(z.chan, z.rows_x, z.tiles, z.rows_y, LANES)
        return shaped.transpose(0, 1, 3, 2, 4).reshape(fields.shape)

    weights = lax.optimization_barrier(spectral.transpose(0, 3, 4, 5, 2, 1).reshape(-1, z.qb))
    weights = jnp.pad(weights, ((0, 0), (0, up(z.qb, LANES) - z.qb)))
    spread = np.kron(np.eye(z.chan), np.ones((z.rows_x, 1))).astype(np.float32)
    same_x = np.kron(np.ones((z.chan, z.chan)), np.eye(z.rows_x)).astype(np.float32)
    x_cols = z.nx * 2 * z.cp
    vmem = pl.BlockSpec(memory_space=pltpu.VMEM)
    hbm = pl.BlockSpec(memory_space=pltpu.HBM)
    any_space = pl.BlockSpec(memory_space=pl.ANY)
    grid_rows = z.cx * z.rows_y * z.tiles
    y_block = (4, z.ny, z.mb2, z.rows_y * z.cp)
    x_block = (4, z.nx, 2 * z.qbp, z.cp)
    output, field_grad, spec, dual = pl.pallas_call(
        functools.partial(chain, z),
        out_shape=(
            jax.ShapeDtypeStruct((grid_rows, LANES), f32),
            jax.ShapeDtypeStruct((grid_rows, LANES), f32),
            jax.ShapeDtypeStruct((z.spec_rows, z.qb), f32),
            jax.ShapeDtypeStruct((z.spec_rows, z.qb), f32),
        ),
        in_specs=[hbm] * 8,
        out_specs=[hbm] * 4,
        scratch_shapes=[
            pltpu.VMEM((grid_rows, LANES), f32),
            pltpu.VMEM((grid_rows, LANES), f32),
            pltpu.VMEM((z.spec_rows, z.qb), f32),
            pltpu.VMEM((z.spec_rows, z.qb), f32),
            pltpu.VMEM((grid_rows, LANES), f32),
            pltpu.VMEM((grid_rows, LANES), f32),
            pltpu.VMEM((z.ny * z.mb2, z.cells), f32),
            pltpu.VMEM(bypass.shape, f32),
            pltpu.VMEM(spread.shape, f32),
            pltpu.VMEM(same_x.shape, f32),
            pltpu.VMEM(weights.shape, f32),
            pltpu.VMEM((z.spec_rows, x_cols), f32),
            pltpu.VMEM((z.ly, z.mb2, z.cp), f32),
            pltpu.VMEM((z.spec_rows, z.qb), f32),
            pltpu.VMEM((z.rows_y, z.cx, z.cells), f32),
            pltpu.VMEM((z.rows_y, z.cx, z.cells), f32),
            pltpu.VMEM(y_block, f32),
            pltpu.VMEM(y_block, f32),
            pltpu.VMEM(x_block, f32),
            pltpu.VMEM(x_block, f32),
            pltpu.SemaphoreType.DMA((4, z.ny)),
            pltpu.SemaphoreType.DMA((4, z.ny)),
            pltpu.SemaphoreType.DMA((4, z.nx)),
            pltpu.SemaphoreType.DMA((4, z.nx)),
            pltpu.SemaphoreType.DMA((8,)),
            pltpu.SemaphoreType.DMA((4,)),
        ],
        compiler_params=pltpu.CompilerParams(
            collective_id=0, has_side_effects=True, vmem_limit_bytes=61 << 20
        ),
        name="fourier_chain",
    )(
        rows(fields), rows(cotangent), depth_table(z), bypass, spread, same_x, weights, x_table(z)
    )
    local_grad, output, field_grad = pl.pallas_call(
        functools.partial(outer, z),
        out_shape=(
            jax.ShapeDtypeStruct(weights.shape, f32),
            jax.ShapeDtypeStruct((grid_rows, LANES), f32),
            jax.ShapeDtypeStruct((grid_rows, LANES), f32),
        ),
        in_specs=[vmem] * 2 + [any_space] * 2,
        out_specs=[any_space] * 3,
        scratch_shapes=[pltpu.VMEM(weights.shape, f32), pltpu.SemaphoreType.DMA((4,))],
        compiler_params=pltpu.CompilerParams(vmem_limit_bytes=61 << 20),
        name="outer_products",
    )(spec, dual, output, field_grad)
    local_grad = lax.optimization_barrier(local_grad[:, : z.qb]).reshape(-1, 1, z.qb)
    local_grad = lax.optimization_barrier(local_grad)
    spectral_grad = local_grad.reshape(2, z.kx, z.chan, z.chan, 1, z.qb).transpose(0, 5, 4, 1, 2, 3)
    if lax.axis_size("dp") > 1:
        spectral_grad = lax.psum(spectral_grad, "dp")
    return (unrows(output), unrows(field_grad), spectral_grad)


def solution(mesh):
    cells = P("dp", None, "gx", "gy", None)
    weights = P(None, "gx", "gy", None, None, None)
    return jax.shard_map(
        on_device,
        mesh=mesh,
        in_specs=(cells, cells, weights, P()),
        out_specs=(cells, cells, weights),
        check_vma=False,
    )
```

```python
import functools
import math

import jax
import jax.numpy as jnp
import numpy as np
from jax import lax
from jax.experimental import pallas as pl
from jax.experimental.pallas import tpu as pltpu
from jax.sharding import PartitionSpec as P

STEPS = 8
MODES_X = 12
MODES_Y = 12
MODES_Z = 12
MODES_T = 8
LANES = 128
MESH = pl.DeviceIdType.MESH
close = lax.Precision.HIGH
NN = (((1,), (0,)), ((), ()))
NT = (((1,), (1,)), ((), ()))
TN = (((0,), (0,)), ((), ()))


def up(value, step):
    return -(-value // step) * step


def product(left, right, dims):
    return lax.dot_general(left, right, dims, precision=close, preferred_element_type=jnp.float32)


def signed(amount):
    ids = np.arange(amount)
    return np.where(ids < amount // 2, ids, ids - amount)


class Sizes:
    def __init__(self, sample, spectral, size_x, size_y):
        _, self.chan, self.rows_x, self.rows_y, self.cells = sample
        self.nx, self.ny = size_x, size_y
        self.full_x, self.full_y = self.rows_x * size_x, self.rows_y * size_y
        self.count = self.full_x * self.full_y * self.cells
        self.tiles = self.cells // LANES
        self.qb = spectral[1]
        self.kx = spectral[3]
        self.mb = MODES_Z * MODES_T // size_y
        self.ly = MODES_Y
        self.mb2 = up(2 * self.mb, 8)
        self.half = self.mb2 // 2
        self.cx = self.chan * self.rows_x
        self.cp = up(self.cx, LANES)
        self.kp = up(self.kx, 8)
        self.qbp = up(self.qb, 8)
        self.spec_rows = 2 * self.chan * self.kp

    def pieces(self, mode):
        start, stop, found = mode * self.mb, (mode + 1) * self.mb, []
        while start < stop:
            owner = start // self.qb
            rows = min(stop, (owner + 1) * self.qb) - start
            found.append((owner, start - owner * self.qb, start - mode * self.mb, rows))
            start += rows
        return found


def depth_table(z):
    depth = z.cells // STEPS
    modes = np.arange(MODES_Z * MODES_T)
    freq_z, freq_t = signed(MODES_Z)[modes // MODES_T], signed(MODES_T)[modes % MODES_T]
    cell = np.arange(z.cells)
    turns = freq_z[:, None] * (cell // STEPS) * STEPS + freq_t[:, None] * (cell % STEPS) * depth
    angle = (turns % z.cells) * (2.0 * math.pi / z.cells)
    table = np.zeros((z.ny, 2, z.half, z.cells))
    table[:, 0, : z.mb] = np.cos(angle).reshape(z.ny, z.mb, z.cells)
    table[:, 1, : z.mb] = -np.sin(angle).reshape(z.ny, z.mb, z.cells)
    return table.reshape(z.ny * z.mb2, z.cells).astype(np.float32)


def x_table(z):
    angle = (signed(z.kx)[:, None] * np.arange(z.full_x) % z.full_x) * (2.0 * math.pi / z.full_x)
    cosine = np.cos(angle).reshape(z.kx, z.nx, z.rows_x)
    sine = np.sin(angle).reshape(z.kx, z.nx, z.rows_x)
    table = np.zeros((2, z.chan, z.kp, z.nx, 2, z.cp))
    for c in range(z.chan):
        cols = slice(c * z.rows_x, (c + 1) * z.rows_x)
        table[0, c, : z.kx, :, 0, cols] = cosine
        table[0, c, : z.kx, :, 1, cols] = sine
        table[1, c, : z.kx, :, 0, cols] = -sine
        table[1, c, : z.kx, :, 1, cols] = cosine
    return table.reshape(z.spec_rows, z.nx * 2 * z.cp).astype(np.float32)


def chain(
    z, fields_hbm, cotangent_hbm, depth_hbm, bypass_hbm, spread_hbm, same_hbm, w_hbm, x_hbm,
    output_hbm, grad_hbm, spec_hbm, dual_hbm,
    output, field_grad, spec, dual, fields, cotangent, depth, bypass, spread, same_x, w, xt, unit, mixed, signal, direct, sg, rg, sx, rx, gs, gr, xs, xr, load_sems, store_sems,
):
    me_x, me_y = lax.axis_index("gx"), lax.axis_index("gy")
    axes = {"gx": (me_x, z.nx), "gy": (me_y, z.ny)}

    barrier = pltpu.get_barrier_semaphore()
    for axis, (me, n) in axes.items():
        for step in range(1, n):
            pl.semaphore_signal(
                barrier, inc=1, device_id={axis: lax.rem(me + step, n)}, device_id_type=MESH
            )
    loads = {}
    for name, src, dst in (
        ("depth", depth_hbm, depth),
        ("fields", fields_hbm, fields),
        ("bypass", bypass_hbm, bypass),
        ("spread", spread_hbm, spread),
        ("same_x", same_hbm, same_x),
        ("x", x_hbm, xt),
        ("w", w_hbm, w),
        ("cotangent", cotangent_hbm, cotangent),
    ):
        loads[name] = pltpu.make_async_copy(src, dst, load_sems.at[len(loads)])
        loads[name].start()

    stores = []

    def store(src, dst):
        stores.append(pltpu.make_async_copy(src, dst, store_sems.at[len(stores)]))
        stores[-1].start()

    def send(axis, src, dst, send_sem, recv_sem):
        me, n = axes[axis]
        copies = []
        for step in range(1, n):
            peer = lax.rem(me + step, n)
            copy = pltpu.make_async_remote_copy(
                src_ref=src.at[peer],
                dst_ref=dst.at[me],
                send_sem=send_sem.at[step],
                recv_sem=recv_sem.at[step],
                device_id={axis: peer},
                device_id_type=MESH,
            )
            copy.start()
            copies.append(copy)
        dst[me] = src[me]
        return copies

    def send_y(turn):
        return send("gy", sg.at[turn], rg.at[turn], gs.at[turn], gr.at[turn])

    def send_x(turn):
        return send("gx", sx.at[turn], rx.at[turn], xs.at[turn], xr.at[turn])

    def finish(copies):
        for copy in copies:
            copy.wait()

    stride = z.tiles * z.rows_y

    def cells_of(ref, y):
        parts = [ref[pl.ds(t * z.rows_y + y, z.cx, stride=stride), :] for t in range(z.tiles)]
        return jnp.concatenate(parts, axis=1)

    def put_cells(ref, y, value):
        for t in range(z.tiles):
            ref[pl.ds(t * z.rows_y + y, z.cx, stride=stride), :] = value[:, t * LANES : (t + 1) * LANES]

    def lanes(y):
        return slice((y % z.rows_y) * z.cp, (y % z.rows_y + 1) * z.cp)

    def depth_in(turn, y, cells):
        if z.cp > z.cx:
            cells = jnp.concatenate([cells, jnp.zeros((z.cp - z.cx, z.cells), jnp.float32)], axis=0)
        found = product(depth[...], cells, NT)
        for block in range(z.ny):
            sg[turn, block, :, lanes(y)] = found[block * z.mb2 : (block + 1) * z.mb2]

    def depth_out(turn, y):
        held = rg[turn, :, :, lanes(y)].reshape(z.ny * z.mb2, z.cp)
        return product(held, depth[...], TN)[: z.cx]

    first_half = lax.broadcasted_iota(jnp.int32, (z.mb2, z.cp), 0) < z.half
    minus_i = jnp.where(first_half, 1.0, -1.0)

    def times_minus_i(value):
        return pltpu.roll(value, z.half, 0) * minus_i

    def wave(y, f):
        angle = 2.0 * math.pi * ((y * f) % z.full_y) / z.full_y
        return math.cos(angle), math.sin(angle)

    def total(terms):
        out = None
        for factor, value in terms:
            if abs(factor) < 1e-12:
                continue
            term = value if factor == 1.0 else value * factor
            out = term if out is None else out + term
        return out

    mid, top = z.full_y // 2, z.ly // 2

    def y_in(turn):
        at = [rg[turn, y // z.rows_y, :, lanes(y)] for y in range(z.full_y)]
        even = [at[y] if y in (0, mid) else at[y] + at[z.full_y - y] for y in range(mid + 1)]
        odd = [None if y in (0, mid) else at[y] - at[z.full_y - y] for y in range(mid)]

        def put(mode, value):
            for part in range(2):
                for owner, there, here, rows in z.pieces(mode):
                    low, base = part * z.half + here, part * z.qbp + there
                    sx[turn, owner, base : base + rows, :] = value[low : low + rows]

        for f in range(top + 1):
            cosines = total([(wave(y, f)[0], even[y]) for y in range(mid + 1)])
            if f == 0:
                put(0, cosines)
                continue
            sines = times_minus_i(total([(wave(y, f)[1], odd[y]) for y in range(1, mid)]))
            if f < top:
                put(f, cosines + sines)
            put(z.ly - f, cosines - sines)

    def y_out(turn):
        for mode in range(z.ly):
            for part in range(2):
                for owner, there, here, rows in z.pieces(mode):
                    low, base = part * z.half + here, part * z.qbp + there
                    unit[mode, low : low + rows, :] = rx[turn, owner, base : base + rows, :]
        even, odd = [unit[0]], [None]
        for f in range(1, top + 1):
            back = unit[z.ly - f]
            ahead = unit[f] if f < top else None
            even.append(back if ahead is None else ahead + back)
            odd.append(times_minus_i(back if ahead is None else back - ahead))
        for y in range(mid + 1):
            cosines = total([(wave(y, f)[0], even[f]) for f in range(top + 1)])
            sines = total([(wave(y, f)[1], odd[f]) for f in range(1, top + 1)]) if 0 < y < mid else None
            if sines is None:
                sg[turn, y // z.rows_y, :, lanes(y)] = cosines
                continue
            other = z.full_y - y
            sg[turn, y // z.rows_y, :, lanes(y)] = cosines + sines
            sg[turn, other // z.rows_y, :, lanes(other)] = cosines - sines

    def x_in(turn):
        held = [
            rx[turn, s, part * z.qbp : part * z.qbp + z.qb, :]
            for s in range(z.nx)
            for part in range(2)
        ]
        return product(xt[...], jnp.concatenate(held, axis=1), NT)

    def x_out(turn):
        found = product(mixed[...], xt[...], TN)
        for s in range(z.nx):
            for part in range(2):
                col = (2 * s + part) * z.cp
                sx[turn, s, part * z.qbp : part * z.qbp + z.qb, :] = found[:, col : col + z.cp]

    pairs = z.chan * z.chan

    def mix(source, adjoint, scale):
        def weight(part, kx, channel):
            return w[pl.ds((part * z.kx + kx) * pairs + channel * z.chan, z.chan), :]

        def forward(kx, carry):
            real = jnp.zeros((z.chan, z.qb), jnp.float32)
            imag = jnp.zeros((z.chan, z.qb), jnp.float32)
            for c in range(z.chan):
                w_real, w_imag = weight(0, kx, c), weight(1, kx, c)
                s_real = source[pl.ds(c * z.kp + kx, 1), :]
                s_imag = source[pl.ds((z.chan + c) * z.kp + kx, 1), :]
                real = real + s_real * w_real - s_imag * w_imag
                imag = imag + s_imag * w_real + s_real * w_imag
            mixed[pl.ds(kx, z.chan, stride=z.kp), :] = real * scale
            mixed[pl.ds(z.chan * z.kp + kx, z.chan, stride=z.kp), :] = imag * scale
            return carry

        def backward(kx, carry):
            real = source[pl.ds(kx, z.chan, stride=z.kp), :]
            imag = source[pl.ds(z.chan * z.kp + kx, z.chan, stride=z.kp), :]
            for c in range(z.chan):
                w_real, w_imag = weight(0, kx, c), weight(1, kx, c)
                b_real = jnp.sum(w_real * real + w_imag * imag, axis=0, keepdims=True)
                b_imag = jnp.sum(w_real * imag - w_imag * real, axis=0, keepdims=True)
                mixed[pl.ds(c * z.kp + kx, 1), :] = b_real
                mixed[pl.ds((z.chan + c) * z.kp + kx, 1), :] = b_imag
            return carry

        lax.fori_loop(0, z.kx, backward if adjoint else forward, 0)

    loads["depth"].wait()
    loads["fields"].wait()
    for y in range(z.rows_y):
        depth_in(0, y, cells_of(fields, y))
    pl.semaphore_wait(barrier, z.nx + z.ny - 2)
    moving = send_y(0)
    mixed[...] = jnp.zeros_like(mixed)
    if z.half != z.mb:
        unit[...] = jnp.zeros_like(unit)
    for name in ("bypass", "spread", "same_x"):
        loads[name].wait()
    exact = lax.Precision.HIGHEST
    wide = lax.dot_general(spread[...], bypass[...], NN, precision=exact)
    square = lax.dot_general(wide, spread[...], NT, precision=exact) * same_x[...]
    for y in range(z.rows_y):
        direct[y] = product(square, cells_of(fields, y), TN)
    finish(moving)
    y_in(0)
    moving = send_x(0)
    loads["x"].wait()
    finish(moving)
    spec[...] = x_in(0)
    loads["w"].wait()
    mix(spec, False, 1.0 / z.count)
    x_out(1)
    finish(send_x(1))
    y_out(1)
    finish(send_y(1))
    loads["cotangent"].wait()

    root = math.sqrt(2.0 / math.pi)
    for y in range(z.rows_y):
        pre = depth_out(1, y) + direct[y]
        square_pre = pre * pre
        bend = jnp.tanh(root * (pre + 0.044715 * (square_pre * pre)))
        put_cells(output, y, 0.5 * pre * (1.0 + bend))
        slope = 0.5 * (1.0 + bend) + 0.5 * pre * (1.0 - bend * bend) * (
            root * (1.0 + 3.0 * 0.044715 * square_pre)
        )
        back = cells_of(cotangent, y) * slope
        signal[y] = back
        depth_in(2, y, back)

    moving = send_y(2)
    store(spec, spec_hbm)
    store(output, output_hbm)
    for y in range(z.rows_y):
        direct[y] = product(square, signal[y], NN)
    finish(moving)
    y_in(2)
    finish(send_x(2))
    dual[...] = x_in(2) * (1.0 / z.count)
    mix(dual, True, None)
    x_out(3)
    moving = send_x(3)
    store(dual, dual_hbm)
    finish(moving)
    y_out(3)
    finish(send_y(3))
    for y in range(z.rows_y):
        put_cells(field_grad, y, depth_out(3, y) + direct[y])
    store(field_grad, grad_hbm)
    finish(stores)


def outer(z, spec, dual, first, second, grad_hbm, first_out, second_out, grad, sems):
    pairs = z.chan * z.chan
    per_part = z.kx * pairs
    moves = [
        pltpu.make_async_copy(first, first_out, sems.at[0]),
        pltpu.make_async_copy(second, second_out, sems.at[1]),
    ]
    for move in moves:
        move.start()
    for part in range(2):
        sign = 1.0 - 2.0 * part

        def body(kx, carry):
            same = dual[pl.ds(part * z.chan * z.kp + kx, z.chan, stride=z.kp), :]
            cross = dual[pl.ds((1 - part) * z.chan * z.kp + kx, z.chan, stride=z.kp), :] * sign
            for c in range(z.chan):
                real = spec[pl.ds(c * z.kp + kx, 1), :]
                imag = spec[pl.ds((z.chan + c) * z.kp + kx, 1), :]
                at = part * per_part + kx * pairs + c * z.chan
                grad[pl.ds(at, z.chan), : z.qb] = real * same + imag * cross
            return carry

        lax.fori_loop(0, z.kx, body, 0)
        rows = pl.ds(part * per_part, per_part)
        move = pltpu.make_async_copy(grad.at[rows], grad_hbm.at[rows], sems.at[2 + part])
        move.start()
        moves.append(move)
    for move in moves:
        move.wait()


def on_device(fields, cotangent, spectral, bypass):
    z = Sizes(fields.shape, spectral.shape, lax.axis_size("gx"), lax.axis_size("gy"))
    f32 = jnp.float32

    def rows(value):
        shaped = value.reshape(z.chan, z.rows_x, z.rows_y, z.tiles, LANES)
        return shaped.transpose(0, 1, 3, 2, 4).reshape(-1, LANES)

    def unrows(value):
        shaped = value.reshape(z.chan, z.rows_x, z.tiles, z.rows_y, LANES)
        return shaped.transpose(0, 1, 3, 2, 4).reshape(fields.shape)

    weights = spectral.transpose(0, 3, 4, 5, 2, 1).reshape(-1, z.qb)
    wide = (weights.shape[0], up(z.qb, LANES))
    spread = np.kron(np.eye(z.chan), np.ones((z.rows_x, 1))).astype(np.float32)
    same_x = np.kron(np.ones((z.chan, z.chan)), np.eye(z.rows_x)).astype(np.float32)
    x_cols = z.nx * 2 * z.cp
    vmem = pl.BlockSpec(memory_space=pltpu.VMEM)
    hbm = pl.BlockSpec(memory_space=pltpu.HBM)
    any_space = pl.BlockSpec(memory_space=pl.ANY)
    grid_rows = z.cx * z.rows_y * z.tiles
    y_block = (4, z.ny, z.mb2, z.rows_y * z.cp)
    x_block = (4, z.nx, 2 * z.qbp, z.cp)
    output, field_grad, spec, dual = pl.pallas_call(
        functools.partial(chain, z),
        out_shape=(
            jax.ShapeDtypeStruct((grid_rows, LANES), f32),
            jax.ShapeDtypeStruct((grid_rows, LANES), f32),
            jax.ShapeDtypeStruct((z.spec_rows, z.qb), f32),
            jax.ShapeDtypeStruct((z.spec_rows, z.qb), f32),
        ),
        in_specs=[hbm] * 8,
        out_specs=[hbm] * 4,
        scratch_shapes=[
            pltpu.VMEM((grid_rows, LANES), f32),
            pltpu.VMEM((grid_rows, LANES), f32),
            pltpu.VMEM((z.spec_rows, z.qb), f32),
            pltpu.VMEM((z.spec_rows, z.qb), f32),
            pltpu.VMEM((grid_rows, LANES), f32),
            pltpu.VMEM((grid_rows, LANES), f32),
            pltpu.VMEM((z.ny * z.mb2, z.cells), f32),
            pltpu.VMEM(bypass.shape, f32),
            pltpu.VMEM(spread.shape, f32),
            pltpu.VMEM(same_x.shape, f32),
            pltpu.VMEM(weights.shape, f32),
            pltpu.VMEM((z.spec_rows, x_cols), f32),
            pltpu.VMEM((z.ly, z.mb2, z.cp), f32),
            pltpu.VMEM((z.spec_rows, z.qb), f32),
            pltpu.VMEM((z.rows_y, z.cx, z.cells), f32),
            pltpu.VMEM((z.rows_y, z.cx, z.cells), f32),
            pltpu.VMEM(y_block, f32),
            pltpu.VMEM(y_block, f32),
            pltpu.VMEM(x_block, f32),
            pltpu.VMEM(x_block, f32),
            pltpu.SemaphoreType.DMA((4, z.ny)),
            pltpu.SemaphoreType.DMA((4, z.ny)),
            pltpu.SemaphoreType.DMA((4, z.nx)),
            pltpu.SemaphoreType.DMA((4, z.nx)),
            pltpu.SemaphoreType.DMA((8,)),
            pltpu.SemaphoreType.DMA((4,)),
        ],
        compiler_params=pltpu.CompilerParams(
            collective_id=0, has_side_effects=True, vmem_limit_bytes=61 << 20
        ),
        name="fourier_chain",
    )(
        rows(fields), rows(cotangent), depth_table(z), bypass, spread, same_x, weights, x_table(z)
    )
    local_grad, output, field_grad = pl.pallas_call(
        functools.partial(outer, z),
        out_shape=(
            jax.ShapeDtypeStruct(wide, f32),
            jax.ShapeDtypeStruct((grid_rows, LANES), f32),
            jax.ShapeDtypeStruct((grid_rows, LANES), f32),
        ),
        in_specs=[vmem] * 4,
        out_specs=[any_space] * 3,
        scratch_shapes=[pltpu.VMEM(wide, f32), pltpu.SemaphoreType.DMA((4,))],
        compiler_params=pltpu.CompilerParams(vmem_limit_bytes=61 << 20),
        name="outer_products",
    )(spec, dual, output, field_grad)
    local_grad = lax.optimization_barrier(local_grad[:, : z.qb]).reshape(-1, 1, z.qb)
    local_grad = lax.optimization_barrier(local_grad)
    spectral_grad = local_grad.reshape(2, z.kx, z.chan, z.chan, 1, z.qb).transpose(0, 5, 4, 1, 2, 3)
    if lax.axis_size("dp") > 1:
        spectral_grad = lax.psum(spectral_grad, "dp")
    return (unrows(output), unrows(field_grad), spectral_grad)


def solution(mesh):
    cells = P("dp", None, "gx", "gy", None)
    weights = P(None, "gx", "gy", None, None, None)
    return jax.shard_map(
        on_device,
        mesh=mesh,
        in_specs=(cells, cells, weights, P()),
        out_specs=(cells, cells, weights),
        check_vma=False,
    )
```

```python
import functools
import math

import jax
import jax.numpy as jnp
import numpy as np
from jax import lax
from jax.experimental import pallas as pl
from jax.experimental.pallas import tpu as pltpu
from jax.sharding import PartitionSpec as P

STEPS = 8
MODES_X = 12
MODES_Y = 12
MODES_Z = 12
MODES_T = 8
LANES = 128
MESH = pl.DeviceIdType.MESH
close = lax.Precision.HIGH
NN = (((1,), (0,)), ((), ()))
NT = (((1,), (1,)), ((), ()))
TN = (((0,), (0,)), ((), ()))


def up(value, step):
    return -(-value // step) * step


def product(left, right, dims):
    return lax.dot_general(left, right, dims, precision=close, preferred_element_type=jnp.float32)


def signed(amount):
    ids = np.arange(amount)
    return np.where(ids < amount // 2, ids, ids - amount)


class Sizes:
    def __init__(self, sample, spectral, size_x, size_y):
        _, self.chan, self.rows_x, self.rows_y, self.cells = sample
        self.nx, self.ny = size_x, size_y
        self.full_x, self.full_y = self.rows_x * size_x, self.rows_y * size_y
        self.count = self.full_x * self.full_y * self.cells
        self.tiles = self.cells // LANES
        self.qb = spectral[1]
        self.kx = spectral[3]
        self.mb = MODES_Z * MODES_T // size_y
        self.ly = MODES_Y
        self.mb2 = up(2 * self.mb, 8)
        self.half = self.mb2 // 2
        self.cx = self.chan * self.rows_x
        self.cp = up(self.cx, LANES)
        self.kp = up(self.kx, 8)
        self.qbp = up(self.qb, 8)
        self.spec_rows = 2 * self.chan * self.kp

    def pieces(self, mode):
        start, stop, found = mode * self.mb, (mode + 1) * self.mb, []
        while start < stop:
            owner = start // self.qb
            rows = min(stop, (owner + 1) * self.qb) - start
            found.append((owner, start - owner * self.qb, start - mode * self.mb, rows))
            start += rows
        return found


def depth_table(z):
    depth = z.cells // STEPS
    modes = np.arange(MODES_Z * MODES_T)
    freq_z, freq_t = signed(MODES_Z)[modes // MODES_T], signed(MODES_T)[modes % MODES_T]
    cell = np.arange(z.cells)
    turns = freq_z[:, None] * (cell // STEPS) * STEPS + freq_t[:, None] * (cell % STEPS) * depth
    angle = (turns % z.cells) * (2.0 * math.pi / z.cells)
    table = np.zeros((z.ny, 2, z.half, z.cells))
    table[:, 0, : z.mb] = np.cos(angle).reshape(z.ny, z.mb, z.cells)
    table[:, 1, : z.mb] = -np.sin(angle).reshape(z.ny, z.mb, z.cells)
    return table.reshape(z.ny * z.mb2, z.cells).astype(np.float32)


def x_table(z):
    angle = (signed(z.kx)[:, None] * np.arange(z.full_x) % z.full_x) * (2.0 * math.pi / z.full_x)
    cosine = np.cos(angle).reshape(z.kx, z.nx, z.rows_x)
    sine = np.sin(angle).reshape(z.kx, z.nx, z.rows_x)
    table = np.zeros((2, z.chan, z.kp, z.nx, 2, z.cp))
    for c in range(z.chan):
        cols = slice(c * z.rows_x, (c + 1) * z.rows_x)
        table[0, c, : z.kx, :, 0, cols] = cosine
        table[0, c, : z.kx, :, 1, cols] = sine
        table[1, c, : z.kx, :, 0, cols] = -sine
        table[1, c, : z.kx, :, 1, cols] = cosine
    return table.reshape(z.spec_rows, z.nx * 2 * z.cp).astype(np.float32)


def chain(
    z, fields_hbm, cotangent_hbm, depth_hbm, bypass_hbm, spread_hbm, same_hbm, w_hbm, x_hbm,
    output_hbm, grad_hbm, spec_hbm, dual_hbm,
    output, field_grad, spec, dual, fields, cotangent, depth, bypass, spread, same_x, w, xt, unit, mixed, signal, direct, sg, rg, sx, rx, gs, gr, xs, xr, load_sems, store_sems,
):
    me_x, me_y = lax.axis_index("gx"), lax.axis_index("gy")
    axes = {"gx": (me_x, z.nx), "gy": (me_y, z.ny)}

    barrier = pltpu.get_barrier_semaphore()
    for axis, (me, n) in axes.items():
        for step in range(1, n):
            pl.semaphore_signal(
                barrier, inc=1, device_id={axis: lax.rem(me + step, n)}, device_id_type=MESH
            )
    loads = {}
    for name, src, dst in (
        ("depth", depth_hbm, depth),
        ("fields", fields_hbm, fields),
        ("bypass", bypass_hbm, bypass),
        ("spread", spread_hbm, spread),
        ("same_x", same_hbm, same_x),
        ("x", x_hbm, xt),
        ("w", w_hbm, w),
        ("cotangent", cotangent_hbm, cotangent),
    ):
        loads[name] = pltpu.make_async_copy(src, dst, load_sems.at[len(loads)])
        loads[name].start()

    stores = []

    def store(src, dst):
        stores.append(pltpu.make_async_copy(src, dst, store_sems.at[len(stores)]))
        stores[-1].start()

    def send(axis, src, dst, send_sem, recv_sem):
        me, n = axes[axis]
        copies = []
        for step in range(1, n):
            peer = lax.rem(me + step, n)
            copy = pltpu.make_async_remote_copy(
                src_ref=src.at[peer],
                dst_ref=dst.at[me],
                send_sem=send_sem.at[step],
                recv_sem=recv_sem.at[step],
                device_id={axis: peer},
                device_id_type=MESH,
            )
            copy.start()
            copies.append(copy)
        dst[me] = src[me]
        return copies

    def send_y(turn, y):
        return send("gy", sg.at[turn, y], rg.at[turn, y], gs.at[turn, y], gr.at[turn, y])

    def send_x(turn):
        return send("gx", sx.at[turn], rx.at[turn], xs.at[turn], xr.at[turn])

    def finish(copies):
        for copy in copies:
            copy.wait()

    stride = z.tiles * z.rows_y

    def cells_of(ref, y):
        parts = [ref[pl.ds(t * z.rows_y + y, z.cx, stride=stride), :] for t in range(z.tiles)]
        return jnp.concatenate(parts, axis=1)

    def put_cells(ref, y, value):
        for t in range(z.tiles):
            ref[pl.ds(t * z.rows_y + y, z.cx, stride=stride), :] = value[:, t * LANES : (t + 1) * LANES]

    def depth_in(turn, y, cells):
        if z.cp > z.cx:
            cells = jnp.concatenate([cells, jnp.zeros((z.cp - z.cx, z.cells), jnp.float32)], axis=0)
        found = product(depth[...], cells, NT)
        for block in range(z.ny):
            sg[turn, y, block] = found[block * z.mb2 : (block + 1) * z.mb2]

    def depth_out(turn, y):
        held = rg[turn, y].reshape(z.ny * z.mb2, z.cp)
        return product(held, depth[...], TN)[: z.cx]

    first_half = lax.broadcasted_iota(jnp.int32, (z.mb2, z.cp), 0) < z.half
    minus_i = jnp.where(first_half, 1.0, -1.0)

    def times_minus_i(value):
        return pltpu.roll(value, z.half, 0) * minus_i

    def wave(y, f):
        angle = 2.0 * math.pi * ((y * f) % z.full_y) / z.full_y
        return math.cos(angle), math.sin(angle)

    def total(terms):
        out = None
        for factor, value in terms:
            if abs(factor) < 1e-12:
                continue
            term = value if factor == 1.0 else value * factor
            out = term if out is None else out + term
        return out

    mid, top = z.full_y // 2, z.ly // 2

    def y_in(turn):
        at = [rg[turn, y % z.rows_y, y // z.rows_y] for y in range(z.full_y)]
        even = [at[y] if y in (0, mid) else at[y] + at[z.full_y - y] for y in range(mid + 1)]
        odd = [None if y in (0, mid) else at[y] - at[z.full_y - y] for y in range(mid)]

        def put(mode, value):
            for part in range(2):
                for owner, there, here, rows in z.pieces(mode):
                    low, base = part * z.half + here, part * z.qbp + there
                    sx[turn, owner, base : base + rows, :] = value[low : low + rows]

        for f in range(top + 1):
            cosines = total([(wave(y, f)[0], even[y]) for y in range(mid + 1)])
            if f == 0:
                put(0, cosines)
                continue
            sines = times_minus_i(total([(wave(y, f)[1], odd[y]) for y in range(1, mid)]))
            if f < top:
                put(f, cosines + sines)
            put(z.ly - f, cosines - sines)

    def y_out(turn):
        for mode in range(z.ly):
            for part in range(2):
                for owner, there, here, rows in z.pieces(mode):
                    low, base = part * z.half + here, part * z.qbp + there
                    unit[mode, low : low + rows, :] = rx[turn, owner, base : base + rows, :]
        even, odd = [unit[0]], [None]
        for f in range(1, top + 1):
            back = unit[z.ly - f]
            ahead = unit[f] if f < top else None
            even.append(back if ahead is None else ahead + back)
            odd.append(times_minus_i(back if ahead is None else back - ahead))
        made, copies = set(), {}

        def put(y, value):
            sg[turn, y % z.rows_y, y // z.rows_y] = value
            made.add(y)

        for y in sorted(range(mid + 1), key=lambda y: y % z.rows_y):
            cosines = total([(wave(y, f)[0], even[f]) for f in range(top + 1)])
            if y in (0, mid):
                put(y, cosines)
            else:
                sines = total([(wave(y, f)[1], odd[f]) for f in range(1, top + 1)])
                put(y, cosines + sines)
                put(z.full_y - y, cosines - sines)
            for row in range(z.rows_y):
                if row not in copies and made.issuperset(range(row, z.full_y, z.rows_y)):
                    copies[row] = send_y(turn, row)
        return copies

    def x_in(turn):
        held = [
            rx[turn, s, part * z.qbp : part * z.qbp + z.qb, :]
            for s in range(z.nx)
            for part in range(2)
        ]
        return product(xt[...], jnp.concatenate(held, axis=1), NT)

    def x_out(turn):
        found = product(mixed[...], xt[...], TN)
        for s in range(z.nx):
            for part in range(2):
                col = (2 * s + part) * z.cp
                sx[turn, s, part * z.qbp : part * z.qbp + z.qb, :] = found[:, col : col + z.cp]

    pairs = z.chan * z.chan

    def mix(source, adjoint, scale):
        def weight(part, kx, channel):
            return w[pl.ds((part * z.kx + kx) * pairs + channel * z.chan, z.chan), :]

        def forward(kx, carry):
            real = jnp.zeros((z.chan, z.qb), jnp.float32)
            imag = jnp.zeros((z.chan, z.qb), jnp.float32)
            for c in range(z.chan):
                w_real, w_imag = weight(0, kx, c), weight(1, kx, c)
                s_real = source[pl.ds(c * z.kp + kx, 1), :]
                s_imag = source[pl.ds((z.chan + c) * z.kp + kx, 1), :]
                real = real + s_real * w_real - s_imag * w_imag
                imag = imag + s_imag * w_real + s_real * w_imag
            mixed[pl.ds(kx, z.chan, stride=z.kp), :] = real * scale
            mixed[pl.ds(z.chan * z.kp + kx, z.chan, stride=z.kp), :] = imag * scale
            return carry

        def backward(kx, carry):
            real = source[pl.ds(kx, z.chan, stride=z.kp), :]
            imag = source[pl.ds(z.chan * z.kp + kx, z.chan, stride=z.kp), :]
            for c in range(z.chan):
                w_real, w_imag = weight(0, kx, c), weight(1, kx, c)
                b_real = jnp.sum(w_real * real + w_imag * imag, axis=0, keepdims=True)
                b_imag = jnp.sum(w_real * imag - w_imag * real, axis=0, keepdims=True)
                mixed[pl.ds(c * z.kp + kx, 1), :] = b_real
                mixed[pl.ds((z.chan + c) * z.kp + kx, 1), :] = b_imag
            return carry

        lax.fori_loop(0, z.kx, backward if adjoint else forward, 0)

    moving = []
    loads["depth"].wait()
    loads["fields"].wait()
    for y in range(z.rows_y):
        depth_in(0, y, cells_of(fields, y))
        if y == 0:
            pl.semaphore_wait(barrier, z.nx + z.ny - 2)
        moving += send_y(0, y)
    mixed[...] = jnp.zeros_like(mixed)
    if z.half != z.mb:
        unit[...] = jnp.zeros_like(unit)
    for name in ("bypass", "spread", "same_x"):
        loads[name].wait()
    exact = lax.Precision.HIGHEST
    wide = lax.dot_general(spread[...], bypass[...], NN, precision=exact)
    square = lax.dot_general(wide, spread[...], NT, precision=exact) * same_x[...]
    for y in range(z.rows_y):
        direct[y] = product(square, cells_of(fields, y), TN)
    finish(moving)
    y_in(0)
    moving = send_x(0)
    loads["x"].wait()
    finish(moving)
    spec[...] = x_in(0)
    loads["w"].wait()
    mix(spec, False, 1.0 / z.count)
    x_out(1)
    finish(send_x(1))
    arriving = y_out(1)
    loads["cotangent"].wait()

    root = math.sqrt(2.0 / math.pi)
    moving = []
    for y in range(z.rows_y):
        finish(arriving[y])
        pre = depth_out(1, y) + direct[y]
        square_pre = pre * pre
        bend = jnp.tanh(root * (pre + 0.044715 * (square_pre * pre)))
        put_cells(output, y, 0.5 * pre * (1.0 + bend))
        slope = 0.5 * (1.0 + bend) + 0.5 * pre * (1.0 - bend * bend) * (
            root * (1.0 + 3.0 * 0.044715 * square_pre)
        )
        back = cells_of(cotangent, y) * slope
        signal[y] = back
        depth_in(2, y, back)
        moving += send_y(2, y)

    store(spec, spec_hbm)
    store(output, output_hbm)
    for y in range(z.rows_y):
        direct[y] = product(square, signal[y], NN)
    finish(moving)
    y_in(2)
    finish(send_x(2))
    dual[...] = x_in(2) * (1.0 / z.count)
    mix(dual, True, None)
    x_out(3)
    moving = send_x(3)
    store(dual, dual_hbm)
    finish(moving)
    arriving = y_out(3)
    for y in range(z.rows_y):
        finish(arriving[y])
        put_cells(field_grad, y, depth_out(3, y) + direct[y])
    store(field_grad, grad_hbm)
    finish(stores)


def outer(z, spec, dual, first, second, grad_hbm, first_out, second_out, grad, sems):
    pairs = z.chan * z.chan
    per_part = z.kx * pairs
    moves = [
        pltpu.make_async_copy(first, first_out, sems.at[0]),
        pltpu.make_async_copy(second, second_out, sems.at[1]),
    ]
    for move in moves:
        move.start()
    for part in range(2):
        sign = 1.0 - 2.0 * part

        def body(kx, carry):
            same = dual[pl.ds(part * z.chan * z.kp + kx, z.chan, stride=z.kp), :]
            cross = dual[pl.ds((1 - part) * z.chan * z.kp + kx, z.chan, stride=z.kp), :] * sign
            for c in range(z.chan):
                real = spec[pl.ds(c * z.kp + kx, 1), :]
                imag = spec[pl.ds((z.chan + c) * z.kp + kx, 1), :]
                at = part * per_part + kx * pairs + c * z.chan
                grad[pl.ds(at, z.chan), : z.qb] = real * same + imag * cross
            return carry

        lax.fori_loop(0, z.kx, body, 0)
        rows = pl.ds(part * per_part, per_part)
        move = pltpu.make_async_copy(grad.at[rows], grad_hbm.at[rows], sems.at[2 + part])
        move.start()
        moves.append(move)
    for move in moves:
        move.wait()


def on_device(fields, cotangent, spectral, bypass):
    z = Sizes(fields.shape, spectral.shape, lax.axis_size("gx"), lax.axis_size("gy"))
    f32 = jnp.float32

    def rows(value):
        shaped = value.reshape(z.chan, z.rows_x, z.rows_y, z.tiles, LANES)
        return shaped.transpose(0, 1, 3, 2, 4).reshape(-1, LANES)

    def unrows(value):
        shaped = value.reshape(z.chan, z.rows_x, z.tiles, z.rows_y, LANES)
        return shaped.transpose(0, 1, 3, 2, 4).reshape(fields.shape)

    weights = spectral.transpose(0, 3, 4, 5, 2, 1).reshape(-1, z.qb)
    wide = (weights.shape[0], up(z.qb, LANES))
    spread = np.kron(np.eye(z.chan), np.ones((z.rows_x, 1))).astype(np.float32)
    same_x = np.kron(np.ones((z.chan, z.chan)), np.eye(z.rows_x)).astype(np.float32)
    x_cols = z.nx * 2 * z.cp
    vmem = pl.BlockSpec(memory_space=pltpu.VMEM)
    hbm = pl.BlockSpec(memory_space=pltpu.HBM)
    any_space = pl.BlockSpec(memory_space=pl.ANY)
    grid_rows = z.cx * z.rows_y * z.tiles
    y_block = (4, z.rows_y, z.ny, z.mb2, z.cp)
    x_block = (4, z.nx, 2 * z.qbp, z.cp)
    output, field_grad, spec, dual = pl.pallas_call(
        functools.partial(chain, z),
        out_shape=(
            jax.ShapeDtypeStruct((grid_rows, LANES), f32),
            jax.ShapeDtypeStruct((grid_rows, LANES), f32),
            jax.ShapeDtypeStruct((z.spec_rows, z.qb), f32),
            jax.ShapeDtypeStruct((z.spec_rows, z.qb), f32),
        ),
        in_specs=[hbm] * 8,
        out_specs=[hbm] * 4,
        scratch_shapes=[
            pltpu.VMEM((grid_rows, LANES), f32),
            pltpu.VMEM((grid_rows, LANES), f32),
            pltpu.VMEM((z.spec_rows, z.qb), f32),
            pltpu.VMEM((z.spec_rows, z.qb), f32),
            pltpu.VMEM((grid_rows, LANES), f32),
            pltpu.VMEM((grid_rows, LANES), f32),
            pltpu.VMEM((z.ny * z.mb2, z.cells), f32),
            pltpu.VMEM(bypass.shape, f32),
            pltpu.VMEM(spread.shape, f32),
            pltpu.VMEM(same_x.shape, f32),
            pltpu.VMEM(weights.shape, f32),
            pltpu.VMEM((z.spec_rows, x_cols), f32),
            pltpu.VMEM((z.ly, z.mb2, z.cp), f32),
            pltpu.VMEM((z.spec_rows, z.qb), f32),
            pltpu.VMEM((z.rows_y, z.cx, z.cells), f32),
            pltpu.VMEM((z.rows_y, z.cx, z.cells), f32),
            pltpu.VMEM(y_block, f32),
            pltpu.VMEM(y_block, f32),
            pltpu.VMEM(x_block, f32),
            pltpu.VMEM(x_block, f32),
            pltpu.SemaphoreType.DMA((4, z.rows_y, z.ny)),
            pltpu.SemaphoreType.DMA((4, z.rows_y, z.ny)),
            pltpu.SemaphoreType.DMA((4, z.nx)),
            pltpu.SemaphoreType.DMA((4, z.nx)),
            pltpu.SemaphoreType.DMA((8,)),
            pltpu.SemaphoreType.DMA((4,)),
        ],
        compiler_params=pltpu.CompilerParams(
            collective_id=0, has_side_effects=True, vmem_limit_bytes=61 << 20
        ),
        name="fourier_chain",
    )(
        rows(fields), rows(cotangent), depth_table(z), bypass, spread, same_x, weights, x_table(z)
    )
    local_grad, output, field_grad = pl.pallas_call(
        functools.partial(outer, z),
        out_shape=(
            jax.ShapeDtypeStruct(wide, f32),
            jax.ShapeDtypeStruct((grid_rows, LANES), f32),
            jax.ShapeDtypeStruct((grid_rows, LANES), f32),
        ),
        in_specs=[vmem] * 4,
        out_specs=[any_space] * 3,
        scratch_shapes=[pltpu.VMEM(wide, f32), pltpu.SemaphoreType.DMA((4,))],
        compiler_params=pltpu.CompilerParams(vmem_limit_bytes=61 << 20),
        name="outer_products",
    )(spec, dual, output, field_grad)
    local_grad = lax.optimization_barrier(local_grad[:, : z.qb]).reshape(-1, 1, z.qb)
    local_grad = lax.optimization_barrier(local_grad)
    spectral_grad = local_grad.reshape(2, z.kx, z.chan, z.chan, 1, z.qb).transpose(0, 5, 4, 1, 2, 3)
    if lax.axis_size("dp") > 1:
        spectral_grad = lax.psum(spectral_grad, "dp")
    return (unrows(output), unrows(field_grad), spectral_grad)


def solution(mesh):
    cells = P("dp", None, "gx", "gy", None)
    weights = P(None, "gx", "gy", None, None, None)
    return jax.shard_map(
        on_device,
        mesh=mesh,
        in_specs=(cells, cells, weights, P()),
        out_specs=(cells, cells, weights),
        check_vma=False,
    )
```

```python
import functools
import math

import jax
import jax.numpy as jnp
import numpy as np
from jax import lax
from jax.experimental import pallas as pl
from jax.experimental.pallas import tpu as pltpu
from jax.sharding import PartitionSpec as P

STEPS = 8
MODES_X = 12
MODES_Y = 12
MODES_Z = 12
MODES_T = 8
LANES = 128
MESH = pl.DeviceIdType.MESH
close = lax.Precision.HIGH
NN = (((1,), (0,)), ((), ()))
NT = (((1,), (1,)), ((), ()))
TN = (((0,), (0,)), ((), ()))


def up(value, step):
    return -(-value // step) * step


def product(left, right, dims):
    return lax.dot_general(left, right, dims, precision=close, preferred_element_type=jnp.float32)


def signed(amount):
    ids = np.arange(amount)
    return np.where(ids < amount // 2, ids, ids - amount)


class Sizes:
    def __init__(self, sample, spectral, size_x, size_y):
        _, self.chan, self.rows_x, self.rows_y, self.cells = sample
        self.nx, self.ny = size_x, size_y
        self.full_x, self.full_y = self.rows_x * size_x, self.rows_y * size_y
        self.count = self.full_x * self.full_y * self.cells
        self.tiles = self.cells // LANES
        self.qb = spectral[1]
        self.kx = spectral[3]
        self.mb = MODES_Z * MODES_T // size_y
        self.ly = MODES_Y
        self.mb2 = up(2 * self.mb, 8)
        self.half = self.mb2 // 2
        self.cx = self.chan * self.rows_x
        self.cp = up(self.cx, LANES)
        self.kp = up(self.kx, 8)
        self.qbp = up(self.qb, 8)
        self.spec_rows = 2 * self.chan * self.kp

    def pieces(self, mode):
        start, stop, found = mode * self.mb, (mode + 1) * self.mb, []
        while start < stop:
            owner = start // self.qb
            rows = min(stop, (owner + 1) * self.qb) - start
            found.append((owner, start - owner * self.qb, start - mode * self.mb, rows))
            start += rows
        return found


def depth_table(z):
    depth = z.cells // STEPS
    modes = np.arange(MODES_Z * MODES_T)
    freq_z, freq_t = signed(MODES_Z)[modes // MODES_T], signed(MODES_T)[modes % MODES_T]
    cell = np.arange(z.cells)
    turns = freq_z[:, None] * (cell // STEPS) * STEPS + freq_t[:, None] * (cell % STEPS) * depth
    angle = (turns % z.cells) * (2.0 * math.pi / z.cells)
    table = np.zeros((z.ny, 2, z.half, z.cells))
    table[:, 0, : z.mb] = np.cos(angle).reshape(z.ny, z.mb, z.cells)
    table[:, 1, : z.mb] = -np.sin(angle).reshape(z.ny, z.mb, z.cells)
    return table.reshape(z.ny * z.mb2, z.cells).astype(np.float32)


def x_table(z):
    angle = (signed(z.kx)[:, None] * np.arange(z.full_x) % z.full_x) * (2.0 * math.pi / z.full_x)
    cosine = np.cos(angle).reshape(z.kx, z.nx, z.rows_x)
    sine = np.sin(angle).reshape(z.kx, z.nx, z.rows_x)
    table = np.zeros((2, z.chan, z.kp, z.nx, 2, z.cp))
    for c in range(z.chan):
        cols = slice(c * z.rows_x, (c + 1) * z.rows_x)
        table[0, c, : z.kx, :, 0, cols] = cosine
        table[0, c, : z.kx, :, 1, cols] = sine
        table[1, c, : z.kx, :, 0, cols] = -sine
        table[1, c, : z.kx, :, 1, cols] = cosine
    return table.reshape(z.spec_rows, z.nx * 2 * z.cp).astype(np.float32)


def chain(
    z, fields_hbm, cotangent_hbm, depth_hbm, bypass_hbm, spread_hbm, same_hbm, w_hbm, x_hbm,
    output_hbm, grad_hbm, spec_hbm, dual_hbm,
    output, field_grad, spec, dual, fields, cotangent, depth, bypass, spread, same_x, w, xt, unit, mixed, signal, direct, sg, rg, sx, rx, gs, gr, xs, xr, load_sems, store_sems,
):
    me_x, me_y = lax.axis_index("gx"), lax.axis_index("gy")
    axes = {"gx": (me_x, z.nx), "gy": (me_y, z.ny)}

    barrier = pltpu.get_barrier_semaphore()
    for axis, (me, n) in axes.items():
        for step in range(1, n):
            pl.semaphore_signal(
                barrier, inc=1, device_id={axis: lax.rem(me + step, n)}, device_id_type=MESH
            )
    loads = {}
    for name, src, dst in (
        ("depth", depth_hbm, depth),
        ("fields", fields_hbm, fields),
        ("bypass", bypass_hbm, bypass),
        ("spread", spread_hbm, spread),
        ("same_x", same_hbm, same_x),
        ("x", x_hbm, xt),
        ("w", w_hbm, w),
        ("cotangent", cotangent_hbm, cotangent),
    ):
        loads[name] = pltpu.make_async_copy(src, dst, load_sems.at[len(loads)])
        loads[name].start()

    stores = []

    def store(src, dst):
        stores.append(pltpu.make_async_copy(src, dst, store_sems.at[len(stores)]))
        stores[-1].start()

    def send(axis, src, dst, send_sem, recv_sem):
        me, n = axes[axis]
        copies = []
        for step in range(1, n):
            peer = lax.rem(me + step, n)
            copy = pltpu.make_async_remote_copy(
                src_ref=src.at[peer],
                dst_ref=dst.at[me],
                send_sem=send_sem.at[step],
                recv_sem=recv_sem.at[step],
                device_id={axis: peer},
                device_id_type=MESH,
            )
            copy.start()
            copies.append(copy)
        dst[me] = src[me]
        return copies

    def send_y(turn, y):
        return send("gy", sg.at[turn, y], rg.at[turn, y], gs.at[turn, y], gr.at[turn, y])

    def send_x(turn):
        return send("gx", sx.at[turn], rx.at[turn], xs.at[turn], xr.at[turn])

    def finish(copies):
        for copy in copies:
            copy.wait()

    stride = z.tiles * z.rows_y

    def cells_of(ref, y):
        parts = [ref[pl.ds(t * z.rows_y + y, z.cx, stride=stride), :] for t in range(z.tiles)]
        return jnp.concatenate(parts, axis=1)

    def put_cells(ref, y, value):
        for t in range(z.tiles):
            ref[pl.ds(t * z.rows_y + y, z.cx, stride=stride), :] = value[:, t * LANES : (t + 1) * LANES]

    def depth_in(turn, y, cells):
        found = product(depth[...], cells, NT)
        for block in range(z.ny):
            sg[turn, y, block] = found[block * z.mb2 : (block + 1) * z.mb2]

    def depth_out(turn, y):
        held = rg[turn, y].reshape(z.ny * z.mb2, z.cx)
        return product(held, depth[...], TN)

    first_half = lax.broadcasted_iota(jnp.int32, (z.mb2, z.cx), 0) < z.half
    minus_i = jnp.where(first_half, 1.0, -1.0)

    def times_minus_i(value):
        return pltpu.roll(value, z.half, 0) * minus_i

    def wave(y, f):
        angle = 2.0 * math.pi * ((y * f) % z.full_y) / z.full_y
        return math.cos(angle), math.sin(angle)

    def total(terms):
        out = None
        for factor, value in terms:
            if abs(factor) < 1e-12:
                continue
            term = value if factor == 1.0 else value * factor
            out = term if out is None else out + term
        return out

    mid, top = z.full_y // 2, z.ly // 2

    def y_in(turn):
        at = [rg[turn, y % z.rows_y, y // z.rows_y] for y in range(z.full_y)]
        even = [at[y] if y in (0, mid) else at[y] + at[z.full_y - y] for y in range(mid + 1)]
        odd = [None if y in (0, mid) else at[y] - at[z.full_y - y] for y in range(mid)]

        def put(mode, value):
            for part in range(2):
                for owner, there, here, rows in z.pieces(mode):
                    low, base = part * z.half + here, part * z.qbp + there
                    sx[turn, owner, base : base + rows, :] = value[low : low + rows]

        for f in range(top + 1):
            cosines = total([(wave(y, f)[0], even[y]) for y in range(mid + 1)])
            if f == 0:
                put(0, cosines)
                continue
            sines = times_minus_i(total([(wave(y, f)[1], odd[y]) for y in range(1, mid)]))
            if f < top:
                put(f, cosines + sines)
            put(z.ly - f, cosines - sines)

    def y_out(turn):
        for mode in range(z.ly):
            for part in range(2):
                for owner, there, here, rows in z.pieces(mode):
                    low, base = part * z.half + here, part * z.qbp + there
                    unit[mode, low : low + rows, :] = rx[turn, owner, base : base + rows, :]
        even, odd = [unit[0]], [None]
        for f in range(1, top + 1):
            back = unit[z.ly - f]
            ahead = unit[f] if f < top else None
            even.append(back if ahead is None else ahead + back)
            odd.append(times_minus_i(back if ahead is None else back - ahead))
        made, copies = set(), {}

        def put(y, value):
            sg[turn, y % z.rows_y, y // z.rows_y] = value
            made.add(y)

        for y in sorted(range(mid + 1), key=lambda y: y % z.rows_y):
            cosines = total([(wave(y, f)[0], even[f]) for f in range(top + 1)])
            if y in (0, mid):
                put(y, cosines)
            else:
                sines = total([(wave(y, f)[1], odd[f]) for f in range(1, top + 1)])
                put(y, cosines + sines)
                put(z.full_y - y, cosines - sines)
            for row in range(z.rows_y):
                if row not in copies and made.issuperset(range(row, z.full_y, z.rows_y)):
                    copies[row] = send_y(turn, row)
        return copies

    def x_in(turn):
        held = [
            rx[turn, s, part * z.qbp : part * z.qbp + z.qb, :]
            for s in range(z.nx)
            for part in range(2)
        ]
        if z.cp > z.cx:
            blank = jnp.zeros((z.qb, z.cp - z.cx), jnp.float32)
            held = [jnp.concatenate([block, blank], axis=1) for block in held]
        return product(xt[...], jnp.concatenate(held, axis=1), NT)

    def x_out(turn):
        found = product(mixed[...], xt[...], TN)
        for s in range(z.nx):
            for part in range(2):
                col = (2 * s + part) * z.cp
                sx[turn, s, part * z.qbp : part * z.qbp + z.qb, :] = found[:, col : col + z.cx]

    pairs = z.chan * z.chan

    def mix(source, adjoint, scale):
        def weight(part, kx, channel):
            return w[pl.ds((part * z.kx + kx) * pairs + channel * z.chan, z.chan), :]

        def forward(kx, carry):
            real = jnp.zeros((z.chan, z.qb), jnp.float32)
            imag = jnp.zeros((z.chan, z.qb), jnp.float32)
            for c in range(z.chan):
                w_real, w_imag = weight(0, kx, c), weight(1, kx, c)
                s_real = source[pl.ds(c * z.kp + kx, 1), :]
                s_imag = source[pl.ds((z.chan + c) * z.kp + kx, 1), :]
                real = real + s_real * w_real - s_imag * w_imag
                imag = imag + s_imag * w_real + s_real * w_imag
            mixed[pl.ds(kx, z.chan, stride=z.kp), :] = real * scale
            mixed[pl.ds(z.chan * z.kp + kx, z.chan, stride=z.kp), :] = imag * scale
            return carry

        def backward(kx, carry):
            real = source[pl.ds(kx, z.chan, stride=z.kp), :]
            imag = source[pl.ds(z.chan * z.kp + kx, z.chan, stride=z.kp), :]
            for c in range(z.chan):
                w_real, w_imag = weight(0, kx, c), weight(1, kx, c)
                b_real = jnp.sum(w_real * real + w_imag * imag, axis=0, keepdims=True)
                b_imag = jnp.sum(w_real * imag - w_imag * real, axis=0, keepdims=True)
                mixed[pl.ds(c * z.kp + kx, 1), :] = b_real
                mixed[pl.ds((z.chan + c) * z.kp + kx, 1), :] = b_imag
            return carry

        lax.fori_loop(0, z.kx, backward if adjoint else forward, 0)

    moving = []
    loads["depth"].wait()
    loads["fields"].wait()
    for y in range(z.rows_y):
        depth_in(0, y, cells_of(fields, y))
        if y == 0:
            pl.semaphore_wait(barrier, z.nx + z.ny - 2)
        moving += send_y(0, y)
    mixed[...] = jnp.zeros_like(mixed)
    if z.half != z.mb:
        unit[...] = jnp.zeros_like(unit)
    for name in ("bypass", "spread", "same_x"):
        loads[name].wait()
    exact = lax.Precision.HIGHEST
    wide = lax.dot_general(spread[...], bypass[...], NN, precision=exact)
    square = lax.dot_general(wide, spread[...], NT, precision=exact) * same_x[...]
    for y in range(z.rows_y):
        direct[y] = product(square, cells_of(fields, y), TN)
    finish(moving)
    y_in(0)
    moving = send_x(0)
    loads["x"].wait()
    finish(moving)
    spec[...] = x_in(0)
    loads["w"].wait()
    mix(spec, False, 1.0 / z.count)
    x_out(1)
    finish(send_x(1))
    arriving = y_out(1)
    loads["cotangent"].wait()

    root = math.sqrt(2.0 / math.pi)
    moving = []
    for y in range(z.rows_y):
        finish(arriving[y])
        pre = depth_out(1, y) + direct[y]
        square_pre = pre * pre
        bend = jnp.tanh(root * (pre + 0.044715 * (square_pre * pre)))
        put_cells(output, y, 0.5 * pre * (1.0 + bend))
        slope = 0.5 * (1.0 + bend) + 0.5 * pre * (1.0 - bend * bend) * (
            root * (1.0 + 3.0 * 0.044715 * square_pre)
        )
        back = cells_of(cotangent, y) * slope
        signal[y] = back
        depth_in(2, y, back)
        moving += send_y(2, y)

    store(spec, spec_hbm)
    store(output, output_hbm)
    for y in range(z.rows_y):
        direct[y] = product(square, signal[y], NN)
    finish(moving)
    y_in(2)
    finish(send_x(2))
    dual[...] = x_in(2) * (1.0 / z.count)
    mix(dual, True, None)
    x_out(3)
    moving = send_x(3)
    store(dual, dual_hbm)
    finish(moving)
    arriving = y_out(3)
    for y in range(z.rows_y):
        finish(arriving[y])
        put_cells(field_grad, y, depth_out(3, y) + direct[y])
    store(field_grad, grad_hbm)
    finish(stores)


def outer(z, spec, dual, first, second, grad_hbm, first_out, second_out, grad, sems):
    pairs = z.chan * z.chan
    per_part = z.kx * pairs
    moves = [
        pltpu.make_async_copy(first, first_out, sems.at[0]),
        pltpu.make_async_copy(second, second_out, sems.at[1]),
    ]
    for move in moves:
        move.start()
    for part in range(2):
        sign = 1.0 - 2.0 * part

        def body(kx, carry):
            same = dual[pl.ds(part * z.chan * z.kp + kx, z.chan, stride=z.kp), :]
            cross = dual[pl.ds((1 - part) * z.chan * z.kp + kx, z.chan, stride=z.kp), :] * sign
            for c in range(z.chan):
                real = spec[pl.ds(c * z.kp + kx, 1), :]
                imag = spec[pl.ds((z.chan + c) * z.kp + kx, 1), :]
                at = part * per_part + kx * pairs + c * z.chan
                grad[pl.ds(at, z.chan), : z.qb] = real * same + imag * cross
            return carry

        lax.fori_loop(0, z.kx, body, 0)
        rows = pl.ds(part * per_part, per_part)
        move = pltpu.make_async_copy(grad.at[rows], grad_hbm.at[rows], sems.at[2 + part])
        move.start()
        moves.append(move)
    for move in moves:
        move.wait()


def on_device(fields, cotangent, spectral, bypass):
    z = Sizes(fields.shape, spectral.shape, lax.axis_size("gx"), lax.axis_size("gy"))
    f32 = jnp.float32

    def rows(value):
        shaped = value.reshape(z.chan, z.rows_x, z.rows_y, z.tiles, LANES)
        return shaped.transpose(0, 1, 3, 2, 4).reshape(-1, LANES)

    def unrows(value):
        shaped = value.reshape(z.chan, z.rows_x, z.tiles, z.rows_y, LANES)
        return shaped.transpose(0, 1, 3, 2, 4).reshape(fields.shape)

    weights = spectral.transpose(0, 3, 4, 5, 2, 1).reshape(-1, z.qb)
    wide = (weights.shape[0], up(z.qb, LANES))
    spread = np.kron(np.eye(z.chan), np.ones((z.rows_x, 1))).astype(np.float32)
    same_x = np.kron(np.ones((z.chan, z.chan)), np.eye(z.rows_x)).astype(np.float32)
    x_cols = z.nx * 2 * z.cp
    vmem = pl.BlockSpec(memory_space=pltpu.VMEM)
    hbm = pl.BlockSpec(memory_space=pltpu.HBM)
    any_space = pl.BlockSpec(memory_space=pl.ANY)
    grid_rows = z.cx * z.rows_y * z.tiles
    y_block = (4, z.rows_y, z.ny, z.mb2, z.cx)
    x_block = (4, z.nx, 2 * z.qbp, z.cx)
    output, field_grad, spec, dual = pl.pallas_call(
        functools.partial(chain, z),
        out_shape=(
            jax.ShapeDtypeStruct((grid_rows, LANES), f32),
            jax.ShapeDtypeStruct((grid_rows, LANES), f32),
            jax.ShapeDtypeStruct((z.spec_rows, z.qb), f32),
            jax.ShapeDtypeStruct((z.spec_rows, z.qb), f32),
        ),
        in_specs=[hbm] * 8,
        out_specs=[hbm] * 4,
        scratch_shapes=[
            pltpu.VMEM((grid_rows, LANES), f32),
            pltpu.VMEM((grid_rows, LANES), f32),
            pltpu.VMEM((z.spec_rows, z.qb), f32),
            pltpu.VMEM((z.spec_rows, z.qb), f32),
            pltpu.VMEM((grid_rows, LANES), f32),
            pltpu.VMEM((grid_rows, LANES), f32),
            pltpu.VMEM((z.ny * z.mb2, z.cells), f32),
            pltpu.VMEM(bypass.shape, f32),
            pltpu.VMEM(spread.shape, f32),
            pltpu.VMEM(same_x.shape, f32),
            pltpu.VMEM(weights.shape, f32),
            pltpu.VMEM((z.spec_rows, x_cols), f32),
            pltpu.VMEM((z.ly, z.mb2, z.cx), f32),
            pltpu.VMEM((z.spec_rows, z.qb), f32),
            pltpu.VMEM((z.rows_y, z.cx, z.cells), f32),
            pltpu.VMEM((z.rows_y, z.cx, z.cells), f32),
            pltpu.VMEM(y_block, f32),
            pltpu.VMEM(y_block, f32),
            pltpu.VMEM(x_block, f32),
            pltpu.VMEM(x_block, f32),
            pltpu.SemaphoreType.DMA((4, z.rows_y, z.ny)),
            pltpu.SemaphoreType.DMA((4, z.rows_y, z.ny)),
            pltpu.SemaphoreType.DMA((4, z.nx)),
            pltpu.SemaphoreType.DMA((4, z.nx)),
            pltpu.SemaphoreType.DMA((8,)),
            pltpu.SemaphoreType.DMA((4,)),
        ],
        compiler_params=pltpu.CompilerParams(
            collective_id=0, has_side_effects=True, vmem_limit_bytes=61 << 20
        ),
        name="fourier_chain",
    )(
        rows(fields), rows(cotangent), depth_table(z), bypass, spread, same_x, weights, x_table(z)
    )
    local_grad, output, field_grad = pl.pallas_call(
        functools.partial(outer, z),
        out_shape=(
            jax.ShapeDtypeStruct(wide, f32),
            jax.ShapeDtypeStruct((grid_rows, LANES), f32),
            jax.ShapeDtypeStruct((grid_rows, LANES), f32),
        ),
        in_specs=[vmem] * 4,
        out_specs=[any_space] * 3,
        scratch_shapes=[pltpu.VMEM(wide, f32), pltpu.SemaphoreType.DMA((4,))],
        compiler_params=pltpu.CompilerParams(vmem_limit_bytes=61 << 20),
        name="outer_products",
    )(spec, dual, output, field_grad)
    local_grad = lax.optimization_barrier(local_grad[:, : z.qb]).reshape(-1, 1, z.qb)
    local_grad = lax.optimization_barrier(local_grad)
    spectral_grad = local_grad.reshape(2, z.kx, z.chan, z.chan, 1, z.qb).transpose(0, 5, 4, 1, 2, 3)
    if lax.axis_size("dp") > 1:
        spectral_grad = lax.psum(spectral_grad, "dp")
    return (unrows(output), unrows(field_grad), spectral_grad)


def solution(mesh):
    cells = P("dp", None, "gx", "gy", None)
    weights = P(None, "gx", "gy", None, None, None)
    return jax.shard_map(
        on_device,
        mesh=mesh,
        in_specs=(cells, cells, weights, P()),
        out_specs=(cells, cells, weights),
        check_vma=False,
    )
```
